32 devices in a mesh: seq: 8 (over z, x), ctx: 4 (over y, core).
Axes of the slice: x: 2, y: 2, z: 4, core: 2. Of those that a mesh axis runs over, the one named last changes fastest.
Arguments:
- hidden_in: bfloat16 [8, 1024, 1024], P('seq', 'ctx'), may hold values from -6 to 6
- segments: int32 [8, 1024], P('seq', 'ctx'), may hold values from 0 to 32, as said below
- positions: int32 [8, 1024], P('seq', 'ctx'), may hold values from 0 to 3070, as said below
- ln1_gain: bfloat16 [1024], P(('seq', 'ctx')), may hold values from 0.5 to 1.5
- ln1_bias: bfloat16 [1024], P(('seq', 'ctx')), may hold values from -1.1953125 to 1.1953125
- ln2_gain: bfloat16 [1024], P(('seq', 'ctx')), may hold values from 0.5 to 1.5
- ln2_bias: bfloat16 [1024], P(('seq', 'ctx')), may hold values from -1.1953125 to 1.1953125
- qkv_weight: bfloat16 [1024, 3072], P(('seq', 'ctx')), may hold values from -0.25 to 0.25
- qkv_bias: bfloat16 [3072], P(('seq', 'ctx')), may hold values from -1.796875 to 1.796875
- out_weight: bfloat16 [1024, 1024], P(('seq', 'ctx')), may hold values from -0.5 to 0.5
- out_bias: bfloat16 [1024], P(('seq', 'ctx')), may hold values from -1.796875 to 1.796875
- up_weight: bfloat16 [1024, 4096], P(('seq', 'ctx')), may hold values from -0.1875 to 0.1875
- up_bias: bfloat16 [4096], P(('seq', 'ctx')), may hold values from -1.796875 to 1.796875
- down_weight: bfloat16 [4096, 1024], P(('seq', 'ctx')), may hold values from -0.09375 to 0.09375
- down_bias: bfloat16 [1024], P(('seq', 'ctx')), may hold values from -1.796875 to 1.796875
- out_grad: bfloat16 [8, 1024, 1024], P('seq', 'ctx'), may hold values from -6 to 6
Outputs:
- hidden_out: bfloat16 [8, 1024, 1024], P('seq', 'ctx')
- input_grad: float32 [8, 1024, 1024], P('seq', 'ctx')
- ln1_gain_grad: float32 [1024], P(('seq', 'ctx'))
- ln1_bias_grad: float32 [1024], P(('seq', 'ctx'))
- ln2_gain_grad: float32 [1024], P(('seq', 'ctx'))
- ln2_bias_grad: float32 [1024], P(('seq', 'ctx'))
- qkv_weight_grad: float32 [1024, 3072], P(('seq', 'ctx'))
- qkv_bias_grad: float32 [3072], P(('seq', 'ctx'))
- out_weight_grad: float32 [1024, 1024], P(('seq', 'ctx'))
- out_bias_grad: float32 [1024], P(('seq', 'ctx'))
- up_weight_grad: float32 [1024, 4096], P(('seq', 'ctx'))
- up_bias_grad: float32 [4096], P(('seq', 'ctx'))
- down_weight_grad: float32 [4096, 1024], P(('seq', 'ctx'))
- down_bias_grad: float32 [1024], P(('seq', 'ctx'))
The draws below stay inside these ranges and needn't reach their ends.
Inputs may be any that keep to these rules, and one draw needn't show every extreme that they name: `segments`: in each row, segment numbers start at 0, never fall, and rise by one at the first token of each document. Within a document, positions rise by one from token to token.
All inputs are finite; a program needn't handle non-finite values.
Results may differ from the reference program's by a relative error of at most 0.012.
The reference program's roundings to bfloat16 on the way count: a program that leaves them out, or rounds other values in their place, can miss the bound.
Values may be sent and summed in bfloat16 or wider, within the bound.
No kernel may reach another device: no remote copies, remote signals or barrier semaphores. Data moves between devices by JAX's collectives and lax.ppermute only.
A program may use at most 192 MiB of HBM per device.

```python
import math
import jax
import jax.numpy as jnp
from jax import lax

D = 1024
H = 16
HD = 64
ROT = 16
FF = 4096
TOK_DEV = 256
LEN = 1024
ROWS = 8


def document_layout(key):
    first_key, second_key, third_key, fourth_key, fifth_key = jax.random.split(key, 5)
    place = jnp.arange(LEN).astype(jnp.int32)[None, :]
    chosen = jax.random.randint(fifth_key, (), 0, ROWS)
    picked = (jnp.arange(ROWS).astype(jnp.int32) == chosen)[:, None]
    head = jax.random.randint(first_key, (ROWS, 1), 1, TOK_DEV // 2 + 1)
    head = jnp.where(picked, TOK_DEV // 2, head)
    tail = LEN - jax.random.randint(second_key, (ROWS, 1), 1, TOK_DEV // 2 + 1)
    tail = jnp.where(picked, LEN - TOK_DEV // 2, tail)
    coin = jax.random.randint(third_key, (ROWS, LEN), 0, 2)
    coin = jnp.where(picked, 1, coin)
    outside = (place < head) | (place > tail)
    starts = (place == head) | (place == tail) | outside & (place % 8 == 0) & (coin == 1) & (place > 0)
    starts = starts.astype(jnp.int32)
    documents = jnp.cumsum(starts, axis=1).astype(jnp.int32)
    begin = lax.cummax(jnp.where(starts == 1, place, 0), axis=1)
    shift_table = jax.random.randint(fourth_key, (ROWS, LEN), 0, 2048)
    offset = jnp.take_along_axis(shift_table, documents, axis=1)
    return (documents, (offset + place - begin).astype(jnp.int32))


def draw_segments(key, part):
    return document_layout(key)[0]


def draw_positions(key, part):
    return document_layout(key)[1]


def block_scale(stream_key, shape, pieces, smallest, high):
    def one(axis_at, parts):
        heights = jax.random.uniform(jax.random.fold_in(jax.random.fold_in(stream_key, 6), axis_at), (parts,), jnp.float32, smallest / len(pieces), high / len(pieces))
        return jnp.repeat(jnp.exp(heights), shape[axis_at] // parts).reshape((-1,) + (1,) * (len(shape) - axis_at - 1))

    factor_of = one(*pieces[0])
    for cut in pieces[1:]:
        factor_of = factor_of * one(*cut)
    return factor_of


def normal_values(own_key, shape, scale, bound, cuts=(), kind=jnp.bfloat16):
    result = jax.random.normal(own_key, shape, jnp.float32) * scale
    if len(cuts) > 0:
        result = block_scale(own_key, shape, cuts, -0.22, 0.18) * result
    return jnp.clip(result, min=-bound, max=bound).astype(kind)


def setup_inputs(seed: int = 0) -> dict:
    arg_keys = jax.random.split(jax.random.key(seed), 17)
    return {
        "hidden_in": normal_values(arg_keys[0], (ROWS, LEN, D), 1.0, 6.0, ((0, 8), (1, 4))),
        "segments": draw_segments(jax.random.fold_in(arg_keys[16], 71), 0),
        "positions": draw_positions(jax.random.fold_in(arg_keys[16], 71), 0),
        "ln1_gain": jnp.clip(1.0 + 0.1 * jax.random.normal(arg_keys[3], (D,), jnp.float32), 0.5, 1.5).astype(jnp.bfloat16),
        "ln1_bias": normal_values(arg_keys[4], (D,), 0.2, 1.1953125, ((0, 32),)),
        "ln2_gain": jnp.clip(1.0 + 0.1 * jax.random.normal(arg_keys[5], (D,), jnp.float32), 0.5, 1.5).astype(jnp.bfloat16),
        "ln2_bias": normal_values(arg_keys[6], (D,), 0.2, 1.1953125, ((0, 32),)),
        "qkv_weight": normal_values(arg_keys[7], (D, 3 * D), (D // 2) ** -0.5, 0.25, ((0, 32),)),
        "qkv_bias": normal_values(arg_keys[8], (3 * D,), 0.3, 1.796875, ((0, 32),)),
        "out_weight": normal_values(arg_keys[9], (D, D), (max(D * 128 // LEN, 1)) ** -0.5, 0.5, ((0, 32),)),
        "out_bias": normal_values(arg_keys[10], (D,), 0.3, 1.796875, ((0, 32),)),
        "up_weight": normal_values(arg_keys[11], (D, FF), D ** -0.5, 0.1875, ((0, 32),)),
        "up_bias": normal_values(arg_keys[12], (FF,), 0.3, 1.796875, ((0, 32),)),
        "down_weight": normal_values(arg_keys[13], (FF, D), FF ** -0.5, 0.09375, ((0, 32),)),
        "down_bias": normal_values(arg_keys[14], (D,), 0.3, 1.796875, ((0, 32),)),
        "out_grad": normal_values(arg_keys[15], (ROWS, LEN, D), 1.0, 6.0, ((0, 8), (1, 4))),
    }


@jax.custom_vjp
def low(v):
    return lax.optimization_barrier(v.astype(jnp.bfloat16)).astype(jnp.float32)

@jax.custom_vjp
def low_back(v):
    return v

def low_keep(v):
    return (low(v), None)

def low_pass(kept, grad):
    return (grad,)

def back_keep(v):
    return (v, None)

def back_low(kept, grad):
    return (low(grad),)
low.defvjp(low_keep, low_pass)
low_back.defvjp(back_keep, back_low)

def product(left, right):
    return jnp.dot(left, right, precision=lax.Precision.HIGHEST)

def norm_layer(value, gain, shift):
    average = lax.optimization_barrier(jnp.mean(value, -1, keepdims=True))
    centred = value - average
    variance = lax.optimization_barrier(jnp.mean(centred * centred, -1, keepdims=True))
    return centred * lax.rsqrt(variance + 1e-05) * gain + shift

def rotate(tensor, cosine, sine):
    half = ROT // 2
    first = tensor[..., :half]
    second = tensor[..., half:ROT]
    cosine = cosine[:, None, :]
    sine = sine[:, None, :]
    return jnp.concatenate([first * cosine - second * sine, second * cosine + first * sine, tensor[..., ROT:]], -1)

def angles(places):
    index = jnp.arange(ROT // 2).astype(jnp.float32)
    frequency = 10000.0 ** (-2.0 * index / ROT)
    turned = places.astype(jnp.float32)[:, None] * frequency[None, :]
    return (jnp.cos(turned), jnp.sin(turned))

def layer(source, params, documents, places):
    gain_one, bias_one, gain_two, bias_two, w_qkv, b_qkv, w_out, b_out, w_up, b_up, w_down, b_down = params
    length = source.shape[0]
    normed_one = low(norm_layer(source, gain_one, bias_one))
    normed_two = low(norm_layer(source, gain_two, bias_two))
    linear = low_back(product(normed_one, w_qkv) + b_qkv).reshape(length, 3, H, HD)
    cosine, sine = angles(places)
    query = low(rotate(linear[:, 0], cosine, sine) * (1.0 / math.sqrt(HD)))
    keys = low(rotate(linear[:, 1], cosine, sine))
    values = low(linear[:, 2])
    block = math.gcd(length, 512)
    key_place = jnp.arange(length).astype(jnp.int32)

    def attend(start):
        rows_here = start + jnp.arange(block).astype(jnp.int32)
        query_block = lax.dynamic_slice_in_dim(query, start, block, 0)
        doc_block = lax.dynamic_slice_in_dim(documents, start, block, 0)
        scores = jnp.einsum('qhd,khd->qhk', query_block, keys, precision=lax.Precision.HIGHEST)
        allowed = (doc_block[:, None] == documents[None, :]) & (rows_here[:, None] >= key_place[None, :])
        scores = low_back(jnp.where(allowed[:, None, :], scores, -1000000000.0))
        prob = low(jax.nn.softmax(scores, axis=-1))
        return jnp.einsum('qhk,khd->qhd', prob, values, precision=lax.Precision.HIGHEST)
    starts = (jnp.arange(length // block) * block).astype(jnp.int32)
    attended = lax.map(jax.checkpoint(attend), starts).reshape(length, H * HD)
    attended = low_back(low(attended))
    branch_attn = product(attended, w_out) + b_out
    upper = low_back(product(normed_two, w_up) + b_up)
    active = low(jax.nn.gelu(upper, approximate=False))
    branch_mlp = product(active, w_down) + b_down
    return source + branch_attn + branch_mlp

def reference(hidden_in, segments, positions, ln1_gain, ln1_bias, ln2_gain, ln2_bias, qkv_weight, qkv_bias, out_weight, out_bias, up_weight, up_bias, down_weight, down_bias, out_grad):
    params = tuple((weight.astype(jnp.float32) for weight in (ln1_gain, ln1_bias, ln2_gain, ln2_bias, qkv_weight, qkv_bias, out_weight, out_bias, up_weight, up_bias, down_weight, down_bias)))

    def one_row(totals, items):
        source, documents, places, cotangent = items

        def forward(inputs, weights):
            return layer(inputs, weights, documents, places)
        output, pull = jax.vjp(forward, source.astype(jnp.float32), params)
        grad_source, grad_params = pull(cotangent.astype(jnp.float32))
        totals = tuple((total + grad for total, grad in zip(totals, grad_params)))
        return (totals, (output.astype(jnp.bfloat16), grad_source))
    zeros = tuple((jnp.zeros_like(weight) for weight in params))
    totals, (hidden_out, input_grad) = lax.scan(one_row, zeros, (hidden_in, segments, positions, out_grad))
    return (hidden_out, input_grad, totals[0], totals[1], totals[2], totals[3], totals[4], totals[5], totals[6], totals[7], totals[8], totals[9], totals[10], totals[11])
```

```python
from functools import partial
import math

import jax
import jax.numpy as jnp
from jax import lax
from jax.experimental import pallas as pl
from jax.experimental.pallas import tpu as pltpu
from jax.sharding import PartitionSpec as P

H = 16
HD = 64
ROT = 16

EPS = 1e-05
NEG = -1000000000.0
BF = jnp.bfloat16
F32 = jnp.float32


def contract_rows(left, right):
    return lax.dot_general(left, right, (((0,), (0,)), ((), ())), preferred_element_type=F32)


def contract_cols(left, right):
    return lax.dot_general(left, right, (((1,), (1,)), ((), ())), preferred_element_type=F32)


def dot(left, right):
    return jnp.dot(left, right, preferred_element_type=F32)


def swap(value, axis, size, bits):
    return lax.ppermute(value, axis, [(i, i ^ bits) for i in range(size)])


def transpose_owner(value, seq, ctx, back=False):
    pairs = [(c * seq + s, s * ctx + c) for s in range(seq) for c in range(ctx)]
    if back:
        pairs = [(b, a) for a, b in pairs]
    return lax.ppermute(value, ("seq", "ctx"), pairs)


def outer_groups(seq):
    return [[2 * z + x for z in range(seq // 2)] for x in range(2)]


def gather_seq(shard, seq, inner):
    own = lax.all_gather(shard, "seq", axis=0, axis_index_groups=outer_groups(seq))
    other = swap(own, "seq", seq, 1)
    first = jnp.where(inner == 0, own, other)
    second = jnp.where(inner == 0, other, own)
    return jnp.stack([first, second], 1).reshape((seq,) + shard.shape)


def scatter_seq(terms, seq, inner):
    split = terms.astype(BF).reshape((seq // 2, 2) + terms.shape[1:])
    sent = lax.dynamic_index_in_dim(split, 1 - inner, 1, keepdims=False)
    kept = lax.dynamic_index_in_dim(split, inner, 1, keepdims=False)
    got = swap(sent, "seq", seq, 1)
    half = (kept.astype(F32) + got.astype(F32)).astype(BF)
    out = lax.psum_scatter(
        half, "seq", scatter_dimension=0, tiled=True, axis_index_groups=outer_groups(seq)
    )
    return out[0]


def gather_ctx(own, ctx):
    even = [own] + [swap(own, "ctx", ctx, k) for k in range(2, ctx, 2)]
    odd = [swap(block, "ctx", ctx, 1) for block in even]
    return even + odd


def natural(blocks, index):
    count = len(blocks)
    half = count // 2
    values = [blocks[(k >> 1) + (k & 1) * half] for k in range(count)]
    bit = 1
    while bit < count:
        on = (index & bit) != 0
        values = [jnp.where(on, values[k ^ bit], values[k]) for k in range(count)]
        bit *= 2
    return values


def scatter_ctx(terms, ctx):
    low = terms.astype(BF)
    half = low.shape[0] // 2
    rows = low.shape[0] // ctx
    got = swap(low[half:], "ctx", ctx, 1)
    pair = low[:half].astype(F32) + got.astype(F32)
    total = pair[:rows]
    for k in range(2, ctx, 2):
        block = pair[(k // 2) * rows : (k // 2 + 1) * rows].astype(BF)
        total = total + swap(block, "ctx", ctx, k).astype(F32)
    return total


def attend_kernel(
    heads,
    ctx,
    spot_ref,
    linear_ref,
    cos_ref,
    sin_ref,
    seg_col_ref,
    seg_row_ref,
    grad_ref,
    out_ref,
    back_ref,
    q_s,
    k_s,
    v_s,
    g_s,
    dq_s,
    dk_s,
    dv_s,
):
    length = linear_ref.shape[0]
    width = grad_ref.shape[1]
    rows = length // ctx
    block = math.gcd(rows, 256)
    scale = 1.0 / math.sqrt(HD)
    lane = lax.broadcasted_iota(jnp.int32, (rows, width), 1) % HD
    low_lane = lane < ROT // 2
    spot = spot_ref[0]

    def place(i):
        other = spot ^ i
        return pl.multiple_of(((other >> 1) + (other & 1) * (ctx // 2)) * rows, rows)

    def turn(u, cosine, sine):
        moved = jnp.where(
            low_lane, pltpu.roll(u, width - ROT // 2, 1), pltpu.roll(u, ROT // 2, 1)
        )
        return u * cosine + moved * sine

    def split(target, value, i):
        low = value.astype(BF)
        for h in range(heads):
            target[h, pl.ds(i * rows, rows), :] = low[:, h * HD : (h + 1) * HD]

    def join(source, i):
        return jnp.concatenate([source[h, pl.ds(i * rows, rows), :] for h in range(heads)], -1)

    def prepare(i, carry):
        at = pl.ds(place(i), rows)
        cosine, sine = cos_ref[at, :], sin_ref[at, :]
        split(q_s, turn(linear_ref[at, 0:width], cosine, sine) * scale, i)
        split(k_s, turn(linear_ref[at, width : 2 * width], cosine, sine), i)
        split(v_s, linear_ref[at, 2 * width : 3 * width], i)
        split(g_s, grad_ref[at, :], i)
        return carry

    lax.fori_loop(0, ctx, prepare, 0)
    dk_s[...] = jnp.zeros_like(dk_s)
    dv_s[...] = jnp.zeros_like(dv_s)

    def one(h, start, size):
        at = pl.ds(start, block)
        query, grad = q_s[h, at, :], g_s[h, at, :]
        keys, values = k_s[h, 0:size, :], v_s[h, 0:size, :]
        scores = contract_cols(query, keys)
        row = start + lax.broadcasted_iota(jnp.int32, (block, size), 0)
        col = lax.broadcasted_iota(jnp.int32, (block, size), 1)
        allowed = (seg_col_ref[at, :] == seg_row_ref[:, 0:size]) & (row >= col)
        scores = jnp.where(allowed, scores, NEG)
        raw = jnp.exp(scores - jnp.max(scores, -1, keepdims=True))
        prob = raw * (1.0 / jnp.sum(raw, -1, keepdims=True))
        prob_low = prob.astype(BF)
        grad_prob = contract_cols(grad, values)
        delta = jnp.sum(prob * grad_prob, -1, keepdims=True)
        grad_score = (prob * (grad_prob - delta)).astype(BF)
        dv_s[h, 0:size, :] += contract_rows(prob_low, grad)
        dk_s[h, 0:size, :] += contract_rows(grad_score, query)
        dq_s[h, at, :] = dot(grad_score, keys)
        q_s[h, at, :] = dot(prob_low, values).astype(BF)

    count = length // block
    if count <= 4:

        def each(h, carry):
            for i in range(count):
                one(h, i * block, (i + 1) * block)
            return carry

        lax.fori_loop(0, heads, each, 0)
    else:

        def each(step, carry):
            one(step // count, pl.multiple_of(step % count * block, block), length)
            return carry

        lax.fori_loop(0, heads * count, each, 0)

    def finish(i, carry):
        at = pl.ds(place(i), rows)
        cosine, sine = cos_ref[at, :], -sin_ref[at, :]
        out_ref[at, :] = join(q_s, i)
        back_ref[at, 0:width] = (turn(join(dq_s, i) * scale, cosine, sine)).astype(BF)
        back_ref[at, width : 2 * width] = turn(join(dk_s, i), cosine, sine).astype(BF)
        back_ref[at, 2 * width : 3 * width] = join(dv_s, i).astype(BF)
        return carry

    lax.fori_loop(0, ctx, finish, 0)


def attend(spot, linear, cosine, sine, seg, grad, heads, ctx):
    length, width = grad.shape
    whole = lambda: pl.BlockSpec(memory_space=pltpu.VMEM)
    shape = (heads, length, HD)
    return pl.pallas_call(
        partial(attend_kernel, heads, ctx),
        out_shape=(
            jax.ShapeDtypeStruct((length, width), BF),
            jax.ShapeDtypeStruct((length, 3 * width), BF),
        ),
        in_specs=[pl.BlockSpec(memory_space=pltpu.SMEM)] + [whole() for _ in range(6)],
        out_specs=(whole(), whole()),
        scratch_shapes=[pltpu.VMEM(shape, BF)] * 4 + [pltpu.VMEM(shape, F32)] * 3,
        compiler_params=pltpu.CompilerParams(vmem_limit_bytes=60 * 1024 * 1024),
        cost_estimate=pl.CostEstimate(
            flops=12 * heads * length * length * HD,
            bytes_accessed=16 * length * width,
            transcendentals=heads * length * length,
        ),
        name="attend",
    )(spot[None], linear, cosine, sine, seg[:, None], seg[None, :], grad)


def local(
    seq,
    ctx,
    hidden_in,
    segments,
    positions,
    ln1_gain,
    ln1_bias,
    ln2_gain,
    ln2_bias,
    qkv_weight,
    qkv_bias,
    out_weight,
    out_bias,
    up_weight,
    up_bias,
    down_weight,
    down_bias,
    out_grad,
):
    spot = lax.axis_index("ctx")
    inner = lax.axis_index("seq") % 2
    tokens, width = hidden_in.shape[1:]
    rows = qkv_weight.shape[0]
    depth = rows * ctx
    hidden = up_weight.shape[1]
    piece = hidden // (seq * ctx)
    share = hidden // ctx
    heads = H // ctx
    part = heads * HD
    source_own = hidden_in[0]
    cotangent_own = out_grad[0]

    out_part = transpose_owner(out_weight, seq, ctx)
    first_shard = jnp.concatenate([down_weight, out_part], 0)
    first = gather_seq(first_shard, seq, inner)

    qkv_cut = qkv_weight.reshape(rows, 3, ctx, part).transpose(2, 0, 1, 3)
    up_cut = up_weight.reshape(rows, seq, ctx, piece).transpose(2, 0, 1, 3)
    ratio = hidden // width
    small = jnp.stack([ln1_gain, ln1_bias, ln2_gain, ln2_bias, out_bias, down_bias], 1)
    small = jnp.concatenate(
        [small, qkv_bias.reshape(rows, 3), up_bias.reshape(rows, ratio)], 1
    )
    count = small.shape[1]
    small = jnp.pad(small, ((0, 0), (0, 128 - count)))
    payload = jnp.concatenate(
        [
            qkv_cut.reshape(ctx, rows, 3 * part),
            up_cut.reshape(ctx, rows, share),
            jnp.broadcast_to(small[None], (ctx, rows, 128)),
        ],
        2,
    )
    payload = lax.all_to_all(payload, "ctx", 0, 0, tiled=True).reshape(depth, -1)
    second = gather_seq(payload[:, 3 * part :], seq, inner)
    third = gather_seq(payload[:, : 3 * part], seq, inner)

    w_down = first[:, : hidden // (seq * ctx)].reshape(share, width)
    w_out = first[:, hidden // (seq * ctx) :].reshape(part, width)
    second = second.reshape(width, share + 128)
    w_up = second[:, :share]
    vectors = second[:, share : share + count]
    gain_one, bias_one, gain_two, bias_two, b_out, b_down = vectors[:, :6].astype(F32).T
    b_qkv = vectors[:, 6:9].reshape(3, ctx, part)
    b_qkv = lax.dynamic_index_in_dim(b_qkv, spot, 1, keepdims=False).reshape(-1).astype(F32)
    b_up = vectors[:, 9:].reshape(seq, ctx, piece)
    b_up = lax.dynamic_index_in_dim(b_up, spot, 1, keepdims=False).reshape(-1).astype(F32)
    w_qkv = third.reshape(width, 3 * part)

    source = jnp.concatenate(gather_ctx(source_own, ctx), 0)
    cotangent = jnp.concatenate(gather_ctx(cotangent_own, ctx), 0)
    marks = gather_ctx(jnp.concatenate([segments, positions], 0), ctx)
    places = jnp.concatenate([mark[1] for mark in marks], 0)
    seg = jnp.concatenate([mark[0] for mark in natural(marks, spot)], 0)

    index = jnp.arange(ROT // 2).astype(F32)
    frequency = 10000.0 ** (-2.0 * index / ROT)
    theta = places.astype(F32)[None, :] * frequency[:, None]
    cosine, sine = jnp.cos(theta), jnp.sin(theta)
    length = places.shape[0]
    cos_wide = jnp.concatenate([cosine, cosine, jnp.ones((HD - ROT, length), F32)], 0)
    sin_wide = jnp.concatenate([-sine, sine, jnp.zeros((HD - ROT, length), F32)], 0)
    cos_wide = jnp.tile(cos_wide.T, (1, heads))
    sin_wide = jnp.tile(sin_wide.T, (1, heads))

    wide = source.astype(F32)
    average = jnp.mean(wide, -1, keepdims=True)
    centred = wide - average
    inverse = lax.rsqrt(jnp.mean(centred * centred, -1, keepdims=True) + EPS)
    unit = centred * inverse
    input_one = (unit * gain_one + bias_one).astype(BF)
    input_two = (unit * gain_two + bias_two).astype(BF)

    grad_active = contract_cols(cotangent, w_down)
    upper = dot(input_two, w_up) + b_up
    cdf = 0.5 * lax.erfc(-upper * math.sqrt(0.5))
    active = (upper * cdf).astype(BF)
    density = jnp.exp(-0.5 * upper * upper) * (1.0 / math.sqrt(2.0 * math.pi))
    upper_low = (grad_active * (cdf + upper * density)).astype(BF)
    down_terms = contract_rows(active, cotangent).reshape(seq, piece, width)
    up_terms = contract_rows(input_two, upper_low).reshape(seq, depth, share)
    grad_down_w = scatter_seq(down_terms, seq, inner).astype(F32)
    up_sum = scatter_seq(up_terms, seq, inner)
    up_back = lax.all_to_all(up_sum.reshape(ctx, rows, share), "ctx", 0, 0, tiled=True)
    grad_up_w = (
        up_back.reshape(ctx, rows, seq, piece).transpose(1, 2, 0, 3).reshape(rows, hidden)
    ).astype(F32)
    grad_up_b = jnp.sum(upper_low.astype(F32), 0)
    branch_mlp = dot(active, w_down)
    grad_two = contract_cols(upper_low, w_up)

    grad_attn = contract_cols(cotangent, w_out).astype(BF)
    linear = dot(input_one, w_qkv) + b_qkv
    attended, grad_linear = attend(
        spot, linear, cos_wide, sin_wide, seg, grad_attn, heads, ctx
    )
    hidden_part = branch_mlp + dot(attended, w_out)
    hidden_sum = scatter_ctx(hidden_part, ctx)
    result = (source_own.astype(F32) + hidden_sum + (b_out + b_down)).astype(BF)[None]

    grad_one = contract_cols(grad_linear, w_qkv)
    qkv_terms = contract_rows(input_one, grad_linear).astype(BF)
    out_terms = contract_rows(attended, cotangent).astype(BF)
    cotangent_full = cotangent_own.astype(F32)
    grad_bias = jnp.sum(cotangent_full, 0)
    grad_qkv_b = jnp.sum(grad_linear.astype(F32), 0).reshape(3, 1, part)
    mine = (jnp.arange(ctx) == spot)[None, :, None]
    grad_qkv_b = jnp.where(mine, grad_qkv_b, 0.0).reshape(width, 3)
    pad_up = (-piece) % depth
    grad_up_b = jnp.pad(grad_up_b.reshape(seq, piece), ((0, 0), (0, pad_up))).reshape(
        seq, -1, depth
    )
    table = jnp.stack(
        [
            jnp.sum(grad_one * unit, 0),
            jnp.sum(grad_one, 0),
            jnp.sum(grad_two * unit, 0),
            jnp.sum(grad_two, 0),
            grad_bias,
        ]
        + [grad_qkv_b[:, k] for k in range(3)]
        + [grad_up_b[:, k].reshape(-1) for k in range(grad_up_b.shape[1])],
        0,
    )
    table = jnp.pad(table, ((0, 128 - table.shape[0]), (0, 0))).T.astype(BF)
    out_rows = part // seq
    cuts = depth // out_rows
    out_terms = out_terms.reshape(seq, out_rows, cuts, width // cuts).transpose(0, 2, 1, 3)
    last = jnp.concatenate(
        [
            qkv_terms.reshape(seq, depth, 3 * part),
            out_terms.reshape(seq, depth, width // cuts),
            table.reshape(seq, depth, 128),
        ],
        2,
    )
    last = scatter_seq(last, seq, inner)
    qkv_sum, out_sum, table = (
        last[:, : 3 * part],
        last[:, 3 * part : 3 * part + width // cuts],
        last[:, 3 * part + width // cuts :],
    )
    out_sum = out_sum.reshape(cuts, out_rows, width // cuts).transpose(1, 0, 2)
    grad_out_w = transpose_owner(
        out_sum.reshape(out_rows, width), seq, ctx, back=True
    ).astype(F32)
    grad_up_b = table[:, 8 : 8 + grad_up_b.shape[1]].T.reshape(-1)[:piece].astype(F32)
    back = jnp.concatenate([qkv_sum, table], 1).reshape(ctx, rows, 3 * part + 128)
    back = lax.all_to_all(back, "ctx", 0, 0, tiled=True)
    grad_qkv_w = (
        back[:, :, : 3 * part]
        .reshape(ctx, rows, 3, part)
        .transpose(1, 2, 0, 3)
        .reshape(rows, 3 * width)
        .astype(F32)
    )
    vectors = jnp.sum(back[:, :, 3 * part :].astype(F32), 0)
    grad_qkv_b = vectors[:, 5:8].reshape(-1)

    flow = scatter_ctx(grad_one * gain_one + grad_two * gain_two, ctx)
    unit_own = unit[:tokens]
    passed = (
        flow
        - jnp.mean(flow, -1, keepdims=True)
        - unit_own * jnp.mean(flow * unit_own, -1, keepdims=True)
    ) * inverse[:tokens]
    input_grad = (cotangent_full + passed)[None]
    return (
        result,
        input_grad,
        vectors[:, 0],
        vectors[:, 1],
        vectors[:, 2],
        vectors[:, 3],
        grad_qkv_w,
        grad_qkv_b,
        grad_out_w,
        vectors[:, 4],
        grad_up_w,
        grad_up_b,
        grad_down_w,
        vectors[:, 4],
    )


def solution(mesh):
    both = P(("seq", "ctx"))
    matrix = P(("seq", "ctx"), None)
    row = P("seq", "ctx", None)
    params = (both, both, both, both, matrix, both, matrix, both, matrix, both, matrix, both)
    in_specs = (row, P("seq", "ctx"), P("seq", "ctx")) + params + (row,)
    out_specs = (row, row) + params
    body = partial(local, mesh.shape["seq"], mesh.shape["ctx"])
    return jax.shard_map(body, mesh=mesh, in_specs=in_specs, out_specs=out_specs, check_vma=False)
```

```python
from functools import partial
import math

import jax
import jax.numpy as jnp
from jax import lax
from jax.experimental import pallas as pl
from jax.experimental.pallas import tpu as pltpu
from jax.sharding import PartitionSpec as P

H = 16
HD = 64
ROT = 16

EPS = 1e-05
NEG = -1000000000.0
BF = jnp.bfloat16
F32 = jnp.float32


def contract_rows(left, right):
    return lax.dot_general(left, right, (((0,), (0,)), ((), ())), preferred_element_type=F32)


def contract_cols(left, right):
    return lax.dot_general(left, right, (((1,), (1,)), ((), ())), preferred_element_type=F32)


def dot(left, right):
    return jnp.dot(left, right, preferred_element_type=F32)


def swap(value, axis, size, bits):
    return lax.ppermute(value, axis, [(i, i ^ bits) for i in range(size)])


class Layout:
    def __init__(self, seq, ctx):
        self.seq, self.ctx = seq, ctx
        self.near = 2 if seq % 2 == 0 and H % (2 * ctx) == 0 else 1
        self.far = seq // self.near
        self.team = self.near * ctx
        self.inner = lax.axis_index("seq") % self.near
        self.spot = lax.axis_index("ctx")
        self.index = self.inner * ctx + self.spot
        self.far_index = lax.axis_index("seq") // self.near
        self.groups = [[self.near * z + x for z in range(self.far)] for x in range(self.near)]

    def gather_far(self, shard):
        return lax.all_gather(shard, "seq", axis=0, axis_index_groups=self.groups)

    def scatter_far(self, terms):
        return lax.psum_scatter(
            terms, "seq", scatter_dimension=0, tiled=True, axis_index_groups=self.groups
        )[0]

    def exchange_near(self, pieces):
        if self.near == 1:
            return pieces[0][:, None]
        mine = lax.dynamic_index_in_dim(pieces, self.inner, 0, keepdims=False)
        sent = lax.dynamic_index_in_dim(pieces, 1 - self.inner, 0, keepdims=False)
        got = swap(sent, "seq", self.seq, 1)
        low = self.inner == 0
        return jnp.stack([jnp.where(low, mine, got), jnp.where(low, got, mine)], 1)

    def exchange(self, pieces):
        return lax.all_to_all(self.exchange_near(pieces), "ctx", 0, 0, tiled=True)

    def own_heads(self, value, back=False):
        pairs = []
        for z in range(self.far):
            for x in range(self.near):
                for c in range(self.ctx):
                    block = (x * self.ctx + c) * self.far + z
                    pairs.append((block, (z * self.near + x) * self.ctx + c))
        if back:
            pairs = [(b, a) for a, b in pairs]
        return lax.ppermute(value, ("seq", "ctx"), pairs)

    def gather_team(self, own, beside, across, route, first=()):
        swap_ctx = lambda v, k: swap(v, "ctx", self.ctx, k)
        if self.near == 1:
            blocks = [own] + across
        elif route == 0:
            blocks = [own, beside]
            for k, block in zip(range(2, self.ctx, 2), across):
                blocks += [block, swap_ctx(beside, k)]
        else:
            blocks = [own, beside]
            for block in across:
                blocks += [block, swap(block, "seq", self.seq, 1)]
        even = after(jnp.concatenate(blocks, 0), *first)
        return even, swap_ctx(even, 1)

    def beside(self, own):
        return swap(own, "seq", self.seq, 1) if self.near == 2 else own

    def across(self, own):
        return [swap(own, "ctx", self.ctx, k) for k in range(2, self.ctx, 2)]

    def spread(self):
        seq_bits = jnp.arange(self.seq) ^ lax.axis_index("seq")
        ctx_bits = jnp.arange(self.ctx) ^ self.spot
        return (ctx_bits[None, :] * self.seq + seq_bits[:, None]).reshape(-1)

    def gather_all(self, vector):
        table = vector[None]
        for axis, size in (("seq", self.seq), ("ctx", self.ctx)):
            bit = 1
            while bit < size:
                table = jnp.concatenate([table, swap(table, axis, size, bit)], 0)
                bit *= 2
        return table[self.spread()]

    def scatter_all(self, table):
        seq_bits = jnp.arange(self.seq) ^ lax.axis_index("seq")
        ctx_bits = jnp.arange(self.ctx) ^ self.spot
        place = (seq_bits[None, :] * self.ctx + ctx_bits[:, None]).reshape(-1)
        table = table[place].reshape(self.ctx, self.seq // 2, 2, -1)
        table = table[:, :, 0] + swap(table[:, :, 1], "seq", self.seq, 1)
        bit = self.ctx // 2
        while bit:
            table = table[:bit] + swap(table[bit:], "ctx", self.ctx, bit)
            bit //= 2
        table = table[0]
        bit = self.seq // 4
        while bit:
            table = table[:bit] + swap(table[bit:], "seq", self.seq, 2 * bit)
            bit //= 2
        return table[0]

    def order(self):
        ks = list(range(0, self.ctx, 2)) + list(range(1, self.ctx, 2))
        return [(x, k) for k in ks for x in range(self.near)]

    def pair_blocks(self, even, got):
        rows = even.shape[0] * 2 // self.team
        width = even.shape[1]
        if self.near == 2 and self.ctx == 4 and width % 256 == 0:
            return list(pair_sums(even, got, rows))
        table = even.astype(F32) + got.astype(F32)
        table = table.reshape(self.ctx // 2, self.near, rows, width)
        return [table[0], table[1:].astype(BF)]

    def scatter_team(self, blocks):
        def over_ctx(kept, sent):
            came = [swap(sent[k - 1], "ctx", self.ctx, 2 * k) for k in range(1, self.ctx // 2)]
            for v in came:
                kept = kept + v.astype(F32)
            return kept, came

        def over_seq(kept, sent):
            came = swap(sent, "seq", self.seq, 1)
            return kept + came.astype(F32), [came]

        kept, first = over_ctx(*blocks[:2])
        if self.near == 2:
            kept, done = over_seq(kept[0], kept[1].astype(BF))
        else:
            kept = kept[0]
        if len(blocks) == 2:
            return kept, first, first
        other, second = over_seq(*blocks[2:])
        other, last = over_ctx(other[0], other[1:].astype(BF))
        done = done + last
        return jnp.concatenate([kept, other], 1), first + second, done


def after(value, *first):
    return lax.optimization_barrier((value,) + first)[0]


def normed(value, gain, shift):
    wide = value.astype(F32)
    centred = wide - jnp.mean(wide, -1, keepdims=True)
    unit = centred * lax.rsqrt(jnp.mean(centred * centred, -1, keepdims=True) + EPS)
    return unit, (unit * gain + shift).astype(BF)


def turn(u, cosine, sine):
    width = u.shape[-1]
    lane = lax.broadcasted_iota(jnp.int32, u.shape, 1) % HD
    moved = jnp.where(
        lane < ROT // 2, pltpu.roll(u, width - ROT // 2, 1), pltpu.roll(u, ROT // 2, 1)
    )
    return u * cosine + moved * sine


def row_sum(value):
    return jnp.sum(value, 0, keepdims=True)


def pack_rows(target, start, size, source, peers):
    rows = source.shape[0] // peers
    depth = target.shape[0] // peers
    for z in range(peers):
        for n in range(source.shape[1] // size):
            at = pl.ds(z * depth + n * rows, rows)
            piece = source[pl.ds(z * rows, rows), pl.ds(n * size, size)]
            target[at, pl.ds(start, size)] = piece.astype(BF)


def mlp_kernel(
    peers, x_ref, g_ref, up_ref, down_ref, gain_ref, shift_ref, bias_ref, gain_one_ref, shift_one_ref,
    hid_ref, flow_ref, one_ref, terms_out, gain_out, shift_out, bias_out,
    down_s, up_s,
):
    step = pl.program_id(0)

    @pl.when(step == 0)
    def _():
        for ref in (down_s, up_s, gain_out, shift_out, bias_out):
            ref[...] = jnp.zeros_like(ref)

    gain = gain_ref[...]
    unit, value = normed(load(x_ref), gain, shift_ref[...])
    one_ref[...] = (unit * gain_one_ref[...] + shift_one_ref[...]).astype(BF)
    grad = load(g_ref)
    upper = dot(value, up_ref[...]) + bias_ref[...]
    grad_active = contract_cols(grad, down_ref[...])
    cdf = 0.5 * (1.0 + lax.erf(upper * math.sqrt(0.5)))
    density = jnp.exp(-0.5 * upper * upper) * (1.0 / math.sqrt(2.0 * math.pi))
    active = (upper * cdf).astype(BF)
    grad_upper = (grad_active * (cdf + upper * density)).astype(BF)
    store(hid_ref, dot(active, down_ref[...]).astype(BF))
    down_s[...] += contract_rows(active, grad)
    up_s[...] += contract_rows(value, grad_upper)
    back = contract_cols(grad_upper, up_ref[...])
    store(flow_ref, (back * gain).astype(BF))
    gain_out[...] += row_sum(back * unit)
    shift_out[...] += row_sum(back)
    bias_out[...] += row_sum(grad_upper.astype(F32))

    @pl.when(step == pl.num_programs(0) - 1)
    def _():
        share = up_s.shape[1]
        terms_out[:, 0:share] = up_s[...].astype(BF)
        pack_rows(terms_out, share, share, down_s, peers)


def head_kernel(
    peers, g_ref, value_ref, cos_ref, sin_ref, third_ref, bias_ref, pack_ref, qkv_ref, out_ref
):
    @pl.when(pl.program_id(0) == 0)
    def _():
        size = third_ref.shape[1] - qkv_ref.shape[1]
        depth, rows = [v.shape[0] // max(peers, 1) for v in (third_ref, out_ref)]
        qkv_ref[...] = third_ref[:, 0 : qkv_ref.shape[1]]
        if not peers:
            out_ref[...] = third_ref[:, qkv_ref.shape[1] :].T
        for z in range(peers):
            for n in range(out_ref.shape[1] // size):
                at = pl.ds(z * depth + n * rows, rows)
                piece = third_ref[at, pl.ds(qkv_ref.shape[1], size)]
                out_ref[pl.ds(z * rows, rows), pl.ds(n * size, size)] = piece

    width = cos_ref.shape[1]
    linear = dot(value_ref[...], qkv_ref[...]) + bias_ref[...]
    cosine, sine = cos_ref[...], sin_ref[...]
    scale = 1.0 / math.sqrt(HD)
    query = turn(linear[:, 0:width], cosine, sine) * scale
    pack_ref[:, 0:width] = query.astype(BF)
    pack_ref[:, width : 2 * width] = turn(linear[:, width : 2 * width], cosine, sine).astype(BF)
    pack_ref[:, 2 * width : 3 * width] = linear[:, 2 * width : 3 * width].astype(BF)
    pack_ref[:, 3 * width : 4 * width] = contract_cols(load(g_ref), out_ref[...]).astype(BF)


def weights_kernel(
    peers, g_ref, value_ref, att_ref, back_ref, cos_ref, sin_ref,
    linear_out, terms_out, bias_out, *rest
):
    *out_out, qkv_s, out_s = rest
    step = pl.program_id(0)
    width = cos_ref.shape[1]

    @pl.when(step == 0)
    def _():
        for ref in (qkv_s, out_s, bias_out):
            ref[...] = jnp.zeros_like(ref)

    cosine, sine = cos_ref[...], -sin_ref[...]
    scale = 1.0 / math.sqrt(HD)
    linear = jnp.concatenate(
        [
            turn(back_ref[:, 0:width] * scale, cosine, sine),
            turn(back_ref[:, width : 2 * width], cosine, sine),
            back_ref[:, 2 * width : 3 * width],
        ],
        -1,
    ).astype(BF)
    linear_out[...] = linear
    qkv_s[...] += contract_rows(value_ref[...], linear)
    out_s[...] += contract_rows(att_ref[...], load(g_ref))
    bias_out[...] += row_sum(linear.astype(F32))

    @pl.when(step == pl.num_programs(0) - 1)
    def _():
        terms_out[:, 0 : 3 * width] = qkv_s[...].astype(BF)
        if peers:
            pack_rows(terms_out, 3 * width, terms_out.shape[1] - 3 * width, out_s, peers)
        else:
            out_out[0][...] = out_s[...].astype(BF)


def flow_kernel(
    x_ref, flow_ref, linear_ref, qkv_ref, gain_ref, shift_ref, flow_out, gain_out, shift_out
):
    @pl.when(pl.program_id(0) == 0)
    def _():
        for ref in (gain_out, shift_out):
            ref[...] = jnp.zeros_like(ref)

    gain = gain_ref[...]
    unit, _ = normed(load(x_ref), gain, shift_ref[...])
    back = contract_cols(linear_ref[...], qkv_ref[...])
    store(flow_out, (load(flow_ref).astype(F32) + back * gain).astype(BF))
    gain_out[...] += row_sum(back * unit)
    shift_out[...] += row_sum(back)


def hidden_kernel(hid_ref, att_ref, out_ref, hid_out):
    store(hid_out, (load(hid_ref).astype(F32) + dot(att_ref[...], out_ref[...])).astype(BF))


def pair_kernel(rows, even_ref, got_ref, left_ref, left_sent, right_ref, right_sent):
    half = even_ref.shape[1] // 2
    for k in range(4):
        at = pl.ds(k * rows, rows)
        total = even_ref[at, :].astype(F32) + got_ref[at, :].astype(F32)
        left, right = total[:, :half], total[:, half:]
        if k < 2:
            left_ref[k] = left
        else:
            left_sent[0, k - 2] = left.astype(BF)
        if k % 2 == 0:
            right_ref[k // 2] = right
        else:
            right_sent[k // 2] = right.astype(BF)


def pair_sums(even, got, rows):
    shape = (2, rows, even.shape[1] // 2)
    return pl.pallas_call(
        partial(pair_kernel, rows),
        out_shape=[
            jax.ShapeDtypeStruct(shape, F32),
            jax.ShapeDtypeStruct((1,) + shape, BF),
            jax.ShapeDtypeStruct(shape, F32),
            jax.ShapeDtypeStruct(shape, BF),
        ],
        in_specs=[pl.BlockSpec(memory_space=pltpu.VMEM)] * 2,
        out_specs=[pl.BlockSpec(memory_space=pltpu.VMEM)] * 4,
        compiler_params=pltpu.CompilerParams(vmem_limit_bytes=60 * 1024 * 1024),
        cost_estimate=pl.CostEstimate(flops=1024, bytes_accessed=1024, transcendentals=0),
        name="pair_sums",
    )(even, got)


def first_half():
    return pl.program_id(0) < pl.num_programs(0) // 2


def load(pair):
    return jnp.where(first_half(), pair[0][...], pair[1][...])


def store(pair, value):
    @pl.when(first_half())
    def _():
        pair[0][...] = value

    @pl.when(jnp.logical_not(first_half()))
    def _():
        pair[1][...] = value


def by_tokens(kernel, tokens, pairs, streamed, fixed, pairs_out, streamed_out, fixed_out, scratch, name):
    block = math.gcd(tokens // 2, 512)
    steps = tokens // block
    stream = lambda n: pl.BlockSpec((block, n), lambda i: (i, 0))
    whole = lambda shape: pl.BlockSpec(shape, lambda i: (0, 0))
    halves = lambda n: [
        pl.BlockSpec((block, n), lambda i: (jnp.minimum(i, steps // 2 - 1), 0)),
        pl.BlockSpec((block, n), lambda i: (jnp.maximum(i - steps // 2, 0), 0)),
    ]
    counts = [2] * len(pairs) + [1] * (len(streamed) + len(fixed))
    counts += [2] * len(pairs_out) + [1] * (len(streamed_out) + len(fixed_out) + len(scratch))

    def body(*refs):
        refs, given = list(refs), []
        for count in counts:
            given.append(refs.pop(0) if count == 1 else (refs.pop(0), refs.pop(0)))
        kernel(*given)

    inputs = [v for pair in pairs for v in pair] + list(streamed) + list(fixed)
    outputs = [jax.ShapeDtypeStruct((tokens // 2, n), BF) for n in pairs_out for _ in range(2)]
    outputs += [jax.ShapeDtypeStruct((tokens, n), BF) for n in streamed_out] + list(fixed_out)
    result = pl.pallas_call(
        body,
        grid=(steps,),
        in_specs=[spec for pair in pairs for spec in halves(pair[0].shape[1])]
        + [stream(v.shape[1]) for v in streamed]
        + [whole(v.shape) for v in fixed],
        out_specs=[spec for n in pairs_out for spec in halves(n)]
        + [stream(n) for n in streamed_out]
        + [whole(v.shape) for v in fixed_out],
        out_shape=outputs,
        scratch_shapes=scratch,
        compiler_params=pltpu.CompilerParams(vmem_limit_bytes=60 * 1024 * 1024),
        cost_estimate=pl.CostEstimate(flops=1024, bytes_accessed=1024, transcendentals=0),
        name=name,
    )(*inputs)
    result, given = list(result), []
    for count in [2] * len(pairs_out) + [1] * (len(streamed_out) + len(fixed_out)):
        given.append(result.pop(0) if count == 1 else (result.pop(0), result.pop(0)))
    return given


def attend_kernel(
    heads, ctx, near,
    spot_ref, pack_ref, seg_col_ref, seg_row_ref,
    out_ref, back_ref,
    q_s, k_s, v_s, g_s, dq_s, dk_s, dv_s,
):
    length = pack_ref.shape[0] // near
    width = out_ref.shape[1]
    rows = length // ctx
    block = math.gcd(rows, 256)
    spot = spot_ref[0]

    def place(i, x):
        other = spot ^ i
        return pl.multiple_of((((other >> 1) + (other & 1) * (ctx // 2)) * near + x) * rows, rows)

    def prepare(step, carry):
        i, x = step // near, step % near
        pack = pack_ref[pl.ds(place(i, x), rows), :]
        for n, target in enumerate((q_s, k_s, v_s, g_s)):
            for h in range(heads):
                low = n * width + h * HD
                target[x * heads + h, pl.ds(i * rows, rows), :] = pack[:, low : low + HD]
        return carry

    lax.fori_loop(0, ctx * near, prepare, 0)
    dk_s[...] = jnp.zeros_like(dk_s)
    dv_s[...] = jnp.zeros_like(dv_s)

    def one(h, start, size):
        at = pl.ds(start, block)
        query, grad = q_s[h, at, :], g_s[h, at, :]
        keys, values = k_s[h, 0:size, :], v_s[h, 0:size, :]
        scores = contract_cols(query, keys)
        row = start + lax.broadcasted_iota(jnp.int32, (block, size), 0)
        col = lax.broadcasted_iota(jnp.int32, (block, size), 1)
        x = h // heads
        seg_col = seg_col_ref[pl.ds(x * length + start, block), :]
        allowed = (seg_col == seg_row_ref[pl.ds(x, 1), 0:size]) & (row >= col)
        scores = jnp.where(allowed, scores, NEG)
        raw = jnp.exp(scores - jnp.max(scores, -1, keepdims=True))
        prob = raw * (1.0 / jnp.sum(raw, -1, keepdims=True))
        prob_low = prob.astype(BF)
        grad_prob = contract_cols(grad, values)
        delta = jnp.sum(prob * grad_prob, -1, keepdims=True)
        grad_score = (prob * (grad_prob - delta)).astype(BF)
        dv_s[h, 0:size, :] += contract_rows(prob_low, grad)
        dk_s[h, 0:size, :] += contract_rows(grad_score, query)
        dq_s[h, at, :] = dot(grad_score, keys)
        q_s[h, at, :] = dot(prob_low, values).astype(BF)

    count = length // block
    if count <= 4:

        def each(h, carry):
            for i in range(count):
                one(h, i * block, (i + 1) * block)
            return carry

        lax.fori_loop(0, near * heads, each, 0)
    else:

        def each(step, carry):
            one(step // count, pl.multiple_of(step % count * block, block), length)
            return carry

        lax.fori_loop(0, near * heads * count, each, 0)

    def finish(step, carry):
        i, x = step // near, step % near
        at = pl.ds(place(i, x), rows)

        def join(source):
            return jnp.concatenate(
                [source[x * heads + h, pl.ds(i * rows, rows), :] for h in range(heads)], -1
            )

        out_ref[at, :] = join(q_s)
        for n, source in enumerate((dq_s, dk_s, dv_s)):
            back_ref[at, n * width : (n + 1) * width] = join(source)
        return carry

    lax.fori_loop(0, ctx * near, finish, 0)


def attend(spot, pack, seg, heads, ctx):
    near = seg.shape[0]
    tokens, width = pack.shape[0], pack.shape[1] // 4
    length = tokens // near
    whole = lambda: pl.BlockSpec(memory_space=pltpu.VMEM)
    shape = (near * heads, length, HD)
    return pl.pallas_call(
        partial(attend_kernel, heads, ctx, near),
        out_shape=(
            jax.ShapeDtypeStruct((tokens, width), BF),
            jax.ShapeDtypeStruct((tokens, 3 * width), F32),
        ),
        in_specs=[pl.BlockSpec(memory_space=pltpu.SMEM)] + [whole() for _ in range(3)],
        out_specs=(whole(), whole()),
        scratch_shapes=[pltpu.VMEM(shape, BF)] * 4 + [pltpu.VMEM(shape, F32)] * 3,
        compiler_params=pltpu.CompilerParams(vmem_limit_bytes=60 * 1024 * 1024),
        cost_estimate=pl.CostEstimate(flops=1024, bytes_accessed=1024, transcendentals=0),
        name="attend",
    )(spot[None], pack, seg.reshape(-1, 1), seg)


def local(
    seq,
    ctx,
    hidden_in,
    segments,
    positions,
    ln1_gain,
    ln1_bias,
    ln2_gain,
    ln2_bias,
    qkv_weight,
    qkv_bias,
    out_weight,
    out_bias,
    up_weight,
    up_bias,
    down_weight,
    down_bias,
    out_grad,
):
    lay = Layout(seq, ctx)
    near, far, team = lay.near, lay.far, lay.team
    tokens, width = hidden_in.shape[1:]
    rows = qkv_weight.shape[0]
    depth = rows * team
    hidden = up_weight.shape[1]
    piece = hidden // (seq * ctx)
    share = hidden // team
    heads = H // team
    part = heads * HD
    out_rows = part // far
    cuts = depth // out_rows
    source_own = hidden_in[0]
    cotangent_own = out_grad[0]

    w_down = lay.gather_far(down_weight).reshape(share, width)

    qkv_cut = qkv_weight.reshape(rows, 3, near, ctx, part).transpose(2, 3, 0, 1, 4)
    up_cut = up_weight.reshape(rows, far, near, ctx, piece).transpose(2, 3, 0, 1, 4)
    payload = jnp.concatenate(
        [qkv_cut.reshape(near, ctx, rows, 3 * part), up_cut.reshape(near, ctx, rows, share)], 3
    )
    payload = lay.exchange_near(payload)
    source_steps = lay.beside(after(source_own, payload)), lay.across(source_own)
    across = lay.across(cotangent_own)
    small = [ln1_gain, ln1_bias, ln2_gain, ln2_bias, out_bias, down_bias, qkv_bias, up_bias]
    small = [v.astype(F32) for v in small + [segments[0], positions[0]]]
    sizes = [v.shape[0] for v in small]
    vectors = lay.gather_all(after(jnp.concatenate(small), payload))
    cut_at = [sum(sizes[:k]) for k in range(len(sizes) + 1)]
    small = [vectors[:, cut_at[k] : cut_at[k + 1]] for k in range(len(sizes))]
    seg, places = small.pop(-2), small.pop(-1)
    small = [v.reshape(-1) for v in small]
    gain_one, bias_one, gain_two, bias_two, b_out, b_down, b_qkv, b_up = small
    b_qkv = lax.dynamic_index_in_dim(b_qkv.reshape(3, team, part), lay.index, 1, keepdims=False)
    b_up = lax.dynamic_index_in_dim(b_up.reshape(far, team, piece), lay.index, 1, keepdims=False)
    seg, places = [
        lax.dynamic_index_in_dim(v.reshape(far, team, tokens), lay.far_index, 0, keepdims=False)
        for v in (seg, places)
    ]
    x_bits = jnp.arange(near)
    seg = seg.reshape(near, ctx * tokens)[x_bits ^ lay.inner].astype(jnp.int32)
    order = jnp.array([(x * ctx + k) for x, k in lay.order()])
    places = places[order ^ lay.index].reshape(-1)

    line = lambda v: v.reshape(1, -1)
    lines = [line(v) for v in (gain_two, bias_two, b_up, gain_one, bias_one, b_qkv)]

    lane = jnp.arange(part) % HD
    frequency = 10000.0 ** (-2.0 * (lane % (ROT // 2)).astype(F32) / ROT)
    frequency = jnp.where(lane < ROT, frequency, 0.0)
    theta = places[:, None] * frequency[None, :]
    cos_wide = jnp.cos(theta)
    sin_wide = jnp.where(lane < ROT // 2, -1.0, 1.0)[None, :] * jnp.sin(theta)

    payload = after(payload, vectors, source_steps[0], *source_steps[1], *across)
    payload = lax.all_to_all(payload, "ctx", 0, 0, tiled=True)
    cotangent_steps = lay.beside(after(cotangent_own, payload)), across
    payload = payload.transpose(1, 0, 2, 3).reshape(depth, -1)
    w_up = lay.gather_far(payload[:, 3 * part :]).reshape(width, share)

    source = lay.gather_team(source_own, *source_steps, 0, [w_down, cos_wide, sin_wide] + lines)
    cotangent = lay.gather_team(cotangent_own, *cotangent_steps, 1)

    out_part = lay.own_heads(after(out_weight, payload))
    out_part = out_part.reshape(out_rows, cuts, width // cuts).transpose(1, 0, 2)
    third = jnp.concatenate([payload[:, : 3 * part], out_part.reshape(depth, -1)], 1)
    third = lay.gather_far(after(third, w_up)).reshape(width, -1)

    count_all = team * tokens
    vector = jax.ShapeDtypeStruct((1, width), F32)

    hid, flow, input_one, terms, gain_two_sum, shift_two_sum, grad_up_b = by_tokens(
        partial(mlp_kernel, far),
        count_all,
        [source, cotangent],
        [],
        [w_up, w_down] + lines[:5],
        [width, width],
        [width],
        [
            jax.ShapeDtypeStruct((width, 2 * share), BF),
            vector,
            vector,
            jax.ShapeDtypeStruct((1, share), F32),
        ],
        [pltpu.VMEM((share, width), F32), pltpu.VMEM((width, share), F32)],
        "feed_forward",
    )
    terms_sum = lay.scatter_far(terms.reshape(far, depth, 2 * share))

    column = width // cuts
    packed = out_rows % 16 == 0 and column % 128 == 0
    if not packed:
        w_out = third[:, 3 * part :].reshape(far, cuts, out_rows, column)
        w_out = w_out.transpose(0, 2, 1, 3).reshape(part, width)
        third = jnp.concatenate([third[:, : 3 * part], w_out.T], 1)
    pack, w_qkv, w_out = by_tokens(
        partial(head_kernel, far if packed else 0),
        count_all,
        [cotangent],
        [input_one, cos_wide, sin_wide],
        [third, lines[5]],
        [],
        [4 * part],
        [jax.ShapeDtypeStruct((width, 3 * part), BF), jax.ShapeDtypeStruct((part, width), BF)],
        [],
        "heads",
    )
    attended, back = attend(lay.spot, pack, seg, heads, ctx)
    (hid,) = by_tokens(
        hidden_kernel, count_all, [hid], [attended], [w_out], [width], [], [], [], "hidden"
    )
    hid_got = swap(hid[1], "ctx", ctx, 1)
    linear, last, grad_qkv_b, *out_terms = by_tokens(
        partial(weights_kernel, far if packed else 0),
        count_all,
        [cotangent],
        [after(input_one, *hid), attended, back, cos_wide, sin_wide],
        [],
        [],
        [3 * part],
        [
            jax.ShapeDtypeStruct((width, 3 * part + packed * column), BF),
            jax.ShapeDtypeStruct((1, 3 * part), F32),
        ]
        + [jax.ShapeDtypeStruct((part, width), BF)] * (not packed),
        [pltpu.VMEM((width, 3 * part), F32), pltpu.VMEM((part, width), F32)],
        "weights",
    )
    last = last.reshape(far, depth, -1)
    if not packed:
        out_terms = out_terms[0].reshape(far, out_rows, cuts, column).transpose(0, 2, 1, 3)
        last = jnp.concatenate([last, out_terms.reshape(far, depth, column)], 2)
    last_sum = lay.scatter_far(after(last, terms_sum))
    hid_first = lay.pair_blocks(after(hid[0], linear), hid_got)
    linear, flow = after((linear, tuple(flow)), terms_sum, *hid_first)
    flow, gain_one_sum, shift_one_sum = by_tokens(
        flow_kernel,
        count_all,
        [source, flow],
        [linear],
        [w_qkv, lines[3], lines[4]],
        [width],
        [],
        [vector, vector],
        [],
        "flow",
    )
    hidden_sum, hid_came, _ = lay.scatter_team(hid_first)
    flow = after(tuple(flow), *hid_came)
    flow_first = lay.pair_blocks(after(flow[0], last_sum), swap(flow[1], "ctx", ctx, 1))
    result = (source_own.astype(F32) + hidden_sum + (b_out + b_down)).astype(BF)[None]

    flow, flow_came, flow_done = lay.scatter_team(flow_first)
    last = after(last_sum, *flow_came)
    terms_sum = after(terms_sum, *flow_came)

    cotangent_full = cotangent_own.astype(F32)
    grad_bias = jnp.sum(cotangent_full, 0)
    mine = (jnp.arange(team) == lay.index)[None, :, None]
    grad_qkv_b = jnp.where(mine, grad_qkv_b.reshape(3, 1, part), 0.0)
    grad_up_b = jnp.where(mine, grad_up_b.reshape(far, 1, piece), 0.0)
    table = [gain_one_sum, shift_one_sum, gain_two_sum, shift_two_sum, grad_bias]
    table = [v.reshape(seq * ctx, -1) for v in table + [grad_qkv_b, grad_up_b]]
    sums = lay.scatter_all(after(jnp.concatenate(table, 1), *flow_came))
    sizes = [v.shape[1] for v in table]
    sums = [sums[sum(sizes[:k]) : sum(sizes[: k + 1])] for k in range(len(sizes))]

    grad_down_w = terms_sum[:, share:].reshape(-1, piece, share)
    grad_down_w = grad_down_w.transpose(1, 0, 2).reshape(piece, width).astype(F32)
    both = jnp.concatenate([last[:, : 3 * part], terms_sum[:, :share]], 1)
    both = lay.exchange(both.reshape(near, ctx, rows, -1))
    grad_up_w = (
        both[..., 3 * part :]
        .reshape(ctx, near, rows, far, piece)
        .transpose(2, 3, 1, 0, 4)
        .reshape(rows, hidden)
        .astype(F32)
    )
    out_sum = last[:, 3 * part :].reshape(cuts, out_rows, width // cuts).transpose(1, 0, 2)
    grad_out_w = lay.own_heads(out_sum.reshape(out_rows, width), back=True).astype(F32)
    grad_qkv_w = (
        both[..., : 3 * part]
        .reshape(ctx, near, rows, 3, part)
        .transpose(2, 3, 1, 0, 4)
        .reshape(rows, 3 * width)
        .astype(F32)
    )

    wide = source_own.astype(F32)
    centred = wide - jnp.mean(wide, -1, keepdims=True)
    inverse = lax.rsqrt(jnp.mean(centred * centred, -1, keepdims=True) + EPS)
    unit = centred * inverse
    passed = (
        flow - jnp.mean(flow, -1, keepdims=True) - unit * jnp.mean(flow * unit, -1, keepdims=True)
    ) * inverse
    input_grad = (cotangent_full + passed)[None]
    return (
        result,
        input_grad,
        sums[0],
        sums[1],
        sums[2],
        sums[3],
        grad_qkv_w,
        sums[5],
        grad_out_w,
        sums[4],
        grad_up_w,
        sums[6],
        grad_down_w,
        sums[4],
    )


def solution(mesh):
    both = P(("seq", "ctx"))
    matrix = P(("seq", "ctx"), None)
    row = P("seq", "ctx", None)
    params = (both, both, both, both, matrix, both, matrix, both, matrix, both, matrix, both)
    in_specs = (row, P("seq", "ctx"), P("seq", "ctx")) + params + (row,)
    out_specs = (row, row) + params
    body = partial(local, mesh.shape["seq"], mesh.shape["ctx"])
    return jax.shard_map(body, mesh=mesh, in_specs=in_specs, out_specs=out_specs, check_vma=False)
```

```python
from functools import partial
import math

import jax
import jax.numpy as jnp
from jax import lax
from jax.experimental import pallas as pl
from jax.experimental.pallas import tpu as pltpu
from jax.sharding import PartitionSpec as P

H = 16
HD = 64
ROT = 16

EPS = 1e-05
NEG = -1000000000.0
BF = jnp.bfloat16
F32 = jnp.float32


def contract_rows(left, right):
    return lax.dot_general(left, right, (((0,), (0,)), ((), ())), preferred_element_type=F32)


def contract_cols(left, right):
    return lax.dot_general(left, right, (((1,), (1,)), ((), ())), preferred_element_type=F32)


def dot(left, right):
    return jnp.dot(left, right, preferred_element_type=F32)


def swap(value, axis, size, bits):
    return lax.ppermute(value, axis, [(i, i ^ bits) for i in range(size)])


class Layout:
    def __init__(self, seq, ctx):
        self.seq, self.ctx = seq, ctx
        self.near = 2 if seq % 2 == 0 and H % (2 * ctx) == 0 else 1
        self.far = seq // self.near
        self.team = self.near * ctx
        self.inner = lax.axis_index("seq") % self.near
        self.spot = lax.axis_index("ctx")
        self.index = self.inner * ctx + self.spot
        self.far_index = lax.axis_index("seq") // self.near
        self.groups = [[self.near * z + x for z in range(self.far)] for x in range(self.near)]

    def gather_far(self, shard):
        return lax.all_gather(shard, "seq", axis=0, axis_index_groups=self.groups)

    def scatter_far(self, terms):
        return lax.psum_scatter(
            terms, "seq", scatter_dimension=0, tiled=True, axis_index_groups=self.groups
        )[0]

    def exchange_near(self, pieces):
        if self.near == 1:
            return pieces[0][:, None]
        mine = lax.dynamic_index_in_dim(pieces, self.inner, 0, keepdims=False)
        sent = lax.dynamic_index_in_dim(pieces, 1 - self.inner, 0, keepdims=False)
        got = swap(sent, "seq", self.seq, 1)
        low = self.inner == 0
        return jnp.stack([jnp.where(low, mine, got), jnp.where(low, got, mine)], 1)

    def exchange(self, pieces):
        return lax.all_to_all(self.exchange_near(pieces), "ctx", 0, 0, tiled=True)

    def own_heads(self, value, back=False):
        pairs = []
        for z in range(self.far):
            for x in range(self.near):
                for c in range(self.ctx):
                    block = (x * self.ctx + c) * self.far + z
                    pairs.append((block, (z * self.near + x) * self.ctx + c))
        if back:
            pairs = [(b, a) for a, b in pairs]
        return lax.ppermute(value, ("seq", "ctx"), pairs)

    def gather_team(self, own, beside, across, route, first=()):
        swap_ctx = lambda v, k: swap(v, "ctx", self.ctx, k)
        if self.near == 1:
            blocks = [own] + across
        elif route == 0:
            blocks = [own, beside]
            for k, block in zip(range(2, self.ctx, 2), across):
                blocks += [block, swap_ctx(beside, k)]
        else:
            blocks = [own, beside]
            for block in across:
                blocks += [block, swap(block, "seq", self.seq, 1)]
        even = after(jnp.concatenate(blocks, 0), *first)
        return even, swap_ctx(even, 1)

    def beside(self, own):
        return swap(own, "seq", self.seq, 1) if self.near == 2 else own

    def across(self, own):
        return [swap(own, "ctx", self.ctx, k) for k in range(2, self.ctx, 2)]

    def spread(self):
        seq_bits = jnp.arange(self.seq) ^ lax.axis_index("seq")
        ctx_bits = jnp.arange(self.ctx) ^ self.spot
        return (ctx_bits[None, :] * self.seq + seq_bits[:, None]).reshape(-1)

    def gather_all(self, vector):
        table = vector[None]
        table = [table] + [swap(table, "seq", self.seq, k) for k in range(2, self.seq, 2)]
        table = jnp.concatenate(table, 0)
        table = jnp.stack([table, swap(table, "seq", self.seq, 1)], 1).reshape(self.seq, -1)
        bit = 1
        while bit < self.ctx:
            table = jnp.concatenate([table, swap(table, "ctx", self.ctx, bit)], 0)
            bit *= 2
        return table[self.spread()]

    def scatter_all_begin(self, table):
        seq_bits = jnp.arange(self.seq) ^ lax.axis_index("seq")
        ctx_bits = jnp.arange(self.ctx) ^ self.spot
        place = (seq_bits[None, :] * self.ctx + ctx_bits[:, None]).reshape(-1)
        table = table[place].reshape(self.ctx // 2, 2, self.seq, -1)
        table = table[:, 0] + swap(table[:, 1], "ctx", self.ctx, 1)
        table = table.reshape(self.ctx // 2, self.seq // 2, 2, -1)
        total = table[:, 0]
        for k in range(1, self.seq // 2):
            total = total + swap(table[:, k], "seq", self.seq, 2 * k)
        return total

    def scatter_all_end(self, table):
        table = table[:, 0] + swap(table[:, 1], "seq", self.seq, 1)
        bit = self.ctx // 4
        while bit:
            table = table[:bit] + swap(table[bit:], "ctx", self.ctx, 2 * bit)
            bit //= 2
        return table[0]

    def order(self):
        ks = list(range(0, self.ctx, 2)) + list(range(1, self.ctx, 2))
        return [(x, k) for k in ks for x in range(self.near)]

    def pair_blocks(self, even, got):
        rows = even.shape[0] * 2 // self.team
        width = even.shape[1]
        if self.near == 2 and self.ctx == 4 and width % 256 == 0:
            return list(pair_sums(even, got, rows))
        table = even.astype(F32) + got.astype(F32)
        table = table.reshape(self.ctx // 2, self.near, rows, width)
        return [table[0], table[1:].astype(BF)]

    def first_steps(self, blocks):
        came = [[swap(blocks[1][k - 1], "ctx", self.ctx, 2 * k) for k in range(1, self.ctx // 2)]]
        if len(blocks) == 4:
            came.append([swap(blocks[3], "seq", self.seq, 1)])
        return came

    def second_steps(self, blocks, came):
        result = []
        for n, values in enumerate(came):
            total = blocks[2 * n]
            for v in values:
                total = total + v.astype(F32)
            result.append((total[0], total[1].astype(BF)) if self.near == 2 else (total[0], None))
        return result

    def last_steps(self, steps):
        if self.near == 1:
            return steps[0][0]
        parts = [steps[0][0] + swap(steps[0][1], "seq", self.seq, 1).astype(F32)]
        if len(steps) == 2:
            parts.append(steps[1][0] + swap(steps[1][1], "ctx", self.ctx, 2).astype(F32))
        return jnp.concatenate(parts, 1)


def after(value, *first):
    return lax.optimization_barrier((value,) + first)[0]


def normed(value, gain, shift):
    wide = value.astype(F32)
    centred = wide - jnp.mean(wide, -1, keepdims=True)
    unit = centred * lax.rsqrt(jnp.mean(centred * centred, -1, keepdims=True) + EPS)
    return unit, (unit * gain + shift).astype(BF)


def turn(u, cosine, sine):
    width = u.shape[-1]
    lane = lax.broadcasted_iota(jnp.int32, u.shape, 1) % HD
    moved = jnp.where(
        lane < ROT // 2, pltpu.roll(u, width - ROT // 2, 1), pltpu.roll(u, ROT // 2, 1)
    )
    return u * cosine + moved * sine


def row_sum(value):
    return jnp.sum(value, 0, keepdims=True)


def pack_rows(target, start, size, source, peers):
    rows = source.shape[0] // peers
    depth = target.shape[0] // peers
    for z in range(peers):
        for n in range(source.shape[1] // size):
            at = pl.ds(z * depth + n * rows, rows)
            piece = source[pl.ds(z * rows, rows), pl.ds(n * size, size)]
            target[at, pl.ds(start, size)] = piece.astype(BF)


def mlp_kernel(
    peers, x_ref, g_ref, up_ref, down_ref, gain_ref, shift_ref, bias_ref, gain_one_ref, shift_one_ref,
    hid_ref, flow_ref, one_ref, terms_out, gain_out, shift_out, bias_out,
    down_s, up_s,
):
    step = pl.program_id(0)

    @pl.when(step == 0)
    def _():
        for ref in (down_s, up_s, gain_out, shift_out, bias_out):
            ref[...] = jnp.zeros_like(ref)

    gain = gain_ref[...]
    source, grad = load(x_ref), load(g_ref)
    half = source.shape[0] // 2
    parts = [slice(0, half), slice(half, 2 * half)]
    stack = lambda values: jnp.concatenate(values, 0)
    units, values = zip(*[normed(source[p], gain, shift_ref[...]) for p in parts])
    uppers = [dot(value, up_ref[...]) + bias_ref[...] for value in values]
    actives, grads = [], []
    for p, upper in zip(parts, uppers):
        grad_active = contract_cols(grad[p], down_ref[...])
        cdf = 0.5 * (1.0 + lax.erf(upper * math.sqrt(0.5)))
        density = jnp.exp(-0.5 * upper * upper) * (1.0 / math.sqrt(2.0 * math.pi))
        actives.append((upper * cdf).astype(BF))
        grads.append((grad_active * (cdf + upper * density)).astype(BF))
    unit, value, active, grad_upper = [stack(v) for v in (units, values, actives, grads)]
    one_ref[...] = (unit * gain_one_ref[...] + shift_one_ref[...]).astype(BF)
    store(hid_ref, dot(active, down_ref[...]).astype(BF))
    down_s[...] += contract_rows(active, grad)
    up_s[...] += contract_rows(value, grad_upper)
    back = contract_cols(grad_upper, up_ref[...])
    store(flow_ref, (back * gain).astype(BF))
    gain_out[...] += row_sum(back * unit)
    shift_out[...] += row_sum(back)
    bias_out[...] += row_sum(grad_upper.astype(F32))

    @pl.when(step == pl.num_programs(0) - 1)
    def _():
        share = up_s.shape[1]
        terms_out[:, 0:share] = up_s[...].astype(BF)
        pack_rows(terms_out, share, share, down_s, peers)


def head_kernel(
    peers, g_ref, value_ref, cos_ref, sin_ref, third_ref, bias_ref, pack_ref, qkv_ref, out_ref
):
    @pl.when(pl.program_id(0) == 0)
    def _():
        size = third_ref.shape[1] - qkv_ref.shape[1]
        depth, rows = [v.shape[0] // max(peers, 1) for v in (third_ref, out_ref)]
        qkv_ref[...] = third_ref[:, 0 : qkv_ref.shape[1]]
        if not peers:
            out_ref[...] = third_ref[:, qkv_ref.shape[1] :].T
        for z in range(peers):
            for n in range(out_ref.shape[1] // size):
                at = pl.ds(z * depth + n * rows, rows)
                piece = third_ref[at, pl.ds(qkv_ref.shape[1], size)]
                out_ref[pl.ds(z * rows, rows), pl.ds(n * size, size)] = piece

    width = cos_ref.shape[1]
    linear = dot(value_ref[...], qkv_ref[...]) + bias_ref[...]
    cosine, sine = cos_ref[...], sin_ref[...]
    scale = 1.0 / math.sqrt(HD)
    query = turn(linear[:, 0:width], cosine, sine) * scale
    pack_ref[:, 0:width] = query.astype(BF)
    pack_ref[:, width : 2 * width] = turn(linear[:, width : 2 * width], cosine, sine).astype(BF)
    pack_ref[:, 2 * width : 3 * width] = linear[:, 2 * width : 3 * width].astype(BF)
    pack_ref[:, 3 * width : 4 * width] = contract_cols(load(g_ref), out_ref[...]).astype(BF)


def weights_kernel(
    peers, g_ref, value_ref, att_ref, back_ref, cos_ref, sin_ref,
    linear_out, terms_out, bias_out, *rest
):
    *out_out, qkv_s, out_s = rest
    step = pl.program_id(0)
    width = cos_ref.shape[1]

    @pl.when(step == 0)
    def _():
        for ref in (qkv_s, out_s, bias_out):
            ref[...] = jnp.zeros_like(ref)

    cosine, sine = cos_ref[...], -sin_ref[...]
    scale = 1.0 / math.sqrt(HD)
    linear = jnp.concatenate(
        [
            turn(back_ref[:, 0:width] * scale, cosine, sine),
            turn(back_ref[:, width : 2 * width], cosine, sine),
            back_ref[:, 2 * width : 3 * width],
        ],
        -1,
    ).astype(BF)
    linear_out[...] = linear
    qkv_s[...] += contract_rows(value_ref[...], linear)
    out_s[...] += contract_rows(att_ref[...], load(g_ref))
    bias_out[...] += row_sum(linear.astype(F32))

    @pl.when(step == pl.num_programs(0) - 1)
    def _():
        terms_out[:, 0 : 3 * width] = qkv_s[...].astype(BF)
        if peers:
            pack_rows(terms_out, 3 * width, terms_out.shape[1] - 3 * width, out_s, peers)
        else:
            out_out[0][...] = out_s[...].astype(BF)


def flow_kernel(
    x_ref, flow_ref, linear_ref, qkv_ref, gain_ref, shift_ref, flow_out, gain_out, shift_out
):
    @pl.when(pl.program_id(0) == 0)
    def _():
        for ref in (gain_out, shift_out):
            ref[...] = jnp.zeros_like(ref)

    gain = gain_ref[...]
    unit, _ = normed(load(x_ref), gain, shift_ref[...])
    back = contract_cols(linear_ref[...], qkv_ref[...])
    store(flow_out, (load(flow_ref).astype(F32) + back * gain).astype(BF))
    gain_out[...] += row_sum(back * unit)
    shift_out[...] += row_sum(back)


def hidden_kernel(hid_ref, att_ref, out_ref, hid_out):
    store(hid_out, (load(hid_ref).astype(F32) + dot(att_ref[...], out_ref[...])).astype(BF))


def pair_kernel(rows, even_ref, got_ref, left_ref, left_sent, right_ref, right_sent):
    half = even_ref.shape[1] // 2
    for k in range(4):
        at = pl.ds(k * rows, rows)
        total = even_ref[at, :].astype(F32) + got_ref[at, :].astype(F32)
        left, right = total[:, :half], total[:, half:]
        if k < 2:
            left_ref[k] = left
        else:
            left_sent[0, k - 2] = left.astype(BF)
        if k % 2 == 0:
            right_ref[k // 2] = right
        else:
            right_sent[k // 2] = right.astype(BF)


def pair_sums(even, got, rows):
    shape = (2, rows, even.shape[1] // 2)
    return pl.pallas_call(
        partial(pair_kernel, rows),
        out_shape=[
            jax.ShapeDtypeStruct(shape, F32),
            jax.ShapeDtypeStruct((1,) + shape, BF),
            jax.ShapeDtypeStruct(shape, F32),
            jax.ShapeDtypeStruct(shape, BF),
        ],
        in_specs=[pl.BlockSpec(memory_space=pltpu.VMEM)] * 2,
        out_specs=[pl.BlockSpec(memory_space=pltpu.VMEM)] * 4,
        compiler_params=pltpu.CompilerParams(vmem_limit_bytes=60 * 1024 * 1024),
        cost_estimate=pl.CostEstimate(flops=1024, bytes_accessed=1024, transcendentals=0),
        name="pair_sums",
    )(even, got)


def unpack_kernel(far, both_ref, qkv_ref, up_ref):
    ctx, near = both_ref.shape[:2]
    team = ctx * near
    part, piece = qkv_ref.shape[1] // (3 * team), up_ref.shape[1] // (far * team)
    for c in range(ctx):
        for x in range(near):
            value = both_ref[c, x].astype(F32)
            for n in range(3):
                at = (n * team + x * ctx + c) * part
                qkv_ref[:, at : at + part] = value[:, n * part : (n + 1) * part]
            for z in range(far):
                at = (z * team + x * ctx + c) * piece
                low = 3 * part + z * piece
                up_ref[:, at : at + piece] = value[:, low : low + piece]


def first_half():
    return pl.program_id(0) < pl.num_programs(0) // 2


def load(pair):
    return jnp.where(first_half(), pair[0][...], pair[1][...])


def store(pair, value):
    @pl.when(first_half())
    def _():
        pair[0][...] = value

    @pl.when(jnp.logical_not(first_half()))
    def _():
        pair[1][...] = value


def by_tokens(kernel, tokens, pairs, streamed, fixed, pairs_out, streamed_out, fixed_out, scratch, name, size=512):
    block = math.gcd(tokens // 2, size)
    steps = tokens // block
    stream = lambda n: pl.BlockSpec((block, n), lambda i: (i, 0))
    whole = lambda shape: pl.BlockSpec(shape, lambda i: (0, 0))
    halves = lambda n: [
        pl.BlockSpec((block, n), lambda i: (jnp.minimum(i, steps // 2 - 1), 0)),
        pl.BlockSpec((block, n), lambda i: (jnp.maximum(i - steps // 2, 0), 0)),
    ]
    counts = [2] * len(pairs) + [1] * (len(streamed) + len(fixed))
    counts += [2] * len(pairs_out) + [1] * (len(streamed_out) + len(fixed_out) + len(scratch))

    def body(*refs):
        refs, given = list(refs), []
        for count in counts:
            given.append(refs.pop(0) if count == 1 else (refs.pop(0), refs.pop(0)))
        kernel(*given)

    inputs = [v for pair in pairs for v in pair] + list(streamed) + list(fixed)
    outputs = [jax.ShapeDtypeStruct((tokens // 2, n), BF) for n in pairs_out for _ in range(2)]
    outputs += [jax.ShapeDtypeStruct((tokens, n), BF) for n in streamed_out] + list(fixed_out)
    result = pl.pallas_call(
        body,
        grid=(steps,),
        in_specs=[spec for pair in pairs for spec in halves(pair[0].shape[1])]
        + [stream(v.shape[1]) for v in streamed]
        + [whole(v.shape) for v in fixed],
        out_specs=[spec for n in pairs_out for spec in halves(n)]
        + [stream(n) for n in streamed_out]
        + [whole(v.shape) for v in fixed_out],
        out_shape=outputs,
        scratch_shapes=scratch,
        compiler_params=pltpu.CompilerParams(vmem_limit_bytes=60 * 1024 * 1024),
        cost_estimate=pl.CostEstimate(flops=1024, bytes_accessed=1024, transcendentals=0),
        name=name,
    )(*inputs)
    result, given = list(result), []
    for count in [2] * len(pairs_out) + [1] * (len(streamed_out) + len(fixed_out)):
        given.append(result.pop(0) if count == 1 else (result.pop(0), result.pop(0)))
    return given


def attend_kernel(
    heads, ctx, near,
    spot_ref, pack_ref, seg_col_ref, seg_row_ref,
    out_ref, back_ref,
    q_s, k_s, v_s, g_s, kt_s, vt_s, dq_s, dk_s, dv_s,
):
    length = pack_ref.shape[0] // near
    width = out_ref.shape[1]
    rows = length // ctx
    block = math.gcd(rows, 256)
    spot = spot_ref[0]

    def place(i, x):
        other = spot ^ i
        return pl.multiple_of((((other >> 1) + (other & 1) * (ctx // 2)) * near + x) * rows, rows)

    def prepare(step, carry):
        i, x = step // near, step % near
        pack = pack_ref[pl.ds(place(i, x), rows), :]
        for n, target in enumerate((q_s, k_s, v_s, g_s)):
            for h in range(heads):
                low = n * width + h * HD
                target[x * heads + h, pl.ds(i * rows, rows), :] = pack[:, low : low + HD]
        return carry

    lax.fori_loop(0, ctx * near, prepare, 0)
    def one(h, start, size):
        at = pl.ds(start, block)
        query, grad = q_s[h, at, :], g_s[h, at, :]
        keys, values = k_s[h, 0:size, :], v_s[h, 0:size, :]
        scores = contract_cols(keys, query)
        row = lax.broadcasted_iota(jnp.int32, (size, block), 0)
        col = start + lax.broadcasted_iota(jnp.int32, (size, block), 1)
        x = h // heads
        seg_col = seg_col_ref[pl.ds(x * length, size), :]
        seg_row = seg_row_ref[pl.ds(x, 1), at]
        scores = jnp.where((seg_col == seg_row) & (row <= col), scores, NEG)
        raw = jnp.exp(scores - jnp.max(scores, 0, keepdims=True))
        prob = raw * (1.0 / jnp.sum(raw, 0, keepdims=True))
        prob_low = prob.astype(BF)
        grad_prob = contract_cols(values, grad)
        delta = jnp.sum(prob * grad_prob, 0, keepdims=True)
        grad_score = (prob * (grad_prob - delta)).astype(BF)
        dv_s[h, 0:size, :] += dot(prob_low, grad)
        dk_s[h, 0:size, :] += dot(grad_score, query)
        dq_s[h, at, :] = dot(kt_s[h, :, 0:size], grad_score).T
        q_s[h, at, :] = dot(vt_s[h, :, 0:size], prob_low).T.astype(BF)

    def flip(h, carry):
        kt_s[h] = k_s[h].T
        vt_s[h] = v_s[h].T
        return carry

    lax.fori_loop(0, near * heads, flip, 0)

    count = length // block
    if count <= 4:

        def each(h, carry):
            x = h // heads
            ats = [pl.ds(i * block, block) for i in range(count)]
            queries, grads = [q_s[h, at, :] for at in ats], [g_s[h, at, :] for at in ats]
            keys, values = k_s[h], v_s[h]
            seg_col = seg_col_ref[pl.ds(pl.multiple_of(x * length, block), length), :]
            seg_row = seg_row_ref[pl.ds(x, 1), :]
            row = lax.broadcasted_iota(jnp.int32, (block, block), 0)
            col = lax.broadcasted_iota(jnp.int32, (block, block), 1)
            scores = [
                contract_cols(keys[: (i + 1) * block], query) for i, query in enumerate(queries)
            ]
            grad_probs = [
                contract_cols(values[: (i + 1) * block], grad) for i, grad in enumerate(grads)
            ]
            probs, grad_scores = [], []
            for i in range(count):
                size = (i + 1) * block
                same = seg_col[:size] == seg_row[:, i * block : size]
                score = jnp.where(same, scores[i], NEG)
                last = jnp.where(row <= col, score[i * block :], NEG)
                score = jnp.concatenate([score[: i * block], last], 0) if i else last
                raw = jnp.exp(score - jnp.max(score, 0, keepdims=True))
                prob = raw * (1.0 / jnp.sum(raw, 0, keepdims=True))
                delta = jnp.sum(prob * grad_probs[i], 0, keepdims=True)
                probs.append(prob.astype(BF))
                grad_scores.append((prob * (grad_probs[i] - delta)).astype(BF))
            for i, at in enumerate(ats):
                size = (i + 1) * block
                dq_s[h, at, :] = dot(kt_s[h, :, 0:size], grad_scores[i]).T
                q_s[h, at, :] = dot(vt_s[h, :, 0:size], probs[i]).T.astype(BF)
            for j, at in enumerate(ats):
                low = slice(j * block, (j + 1) * block)
                dv_s[h, at, :] = sum(dot(probs[i][low], grads[i]) for i in range(j, count))
                dk_s[h, at, :] = sum(dot(grad_scores[i][low], queries[i]) for i in range(j, count))
            return carry

        lax.fori_loop(0, near * heads, each, 0)
    else:
        dk_s[...] = jnp.zeros_like(dk_s)
        dv_s[...] = jnp.zeros_like(dv_s)

        def each(step, carry):
            one(step // count, pl.multiple_of(step % count * block, block), length)
            return carry

        lax.fori_loop(0, near * heads * count, each, 0)

    def finish(step, carry):
        i, x = step // near, step % near
        at = pl.ds(place(i, x), rows)

        def join(source):
            return jnp.concatenate(
                [source[x * heads + h, pl.ds(i * rows, rows), :] for h in range(heads)], -1
            )

        out_ref[at, :] = join(q_s)
        for n, source in enumerate((dq_s, dk_s, dv_s)):
            back_ref[at, n * width : (n + 1) * width] = join(source)
        return carry

    lax.fori_loop(0, ctx * near, finish, 0)


def attend(spot, pack, seg, heads, ctx):
    near = seg.shape[0]
    tokens, width = pack.shape[0], pack.shape[1] // 4
    length = tokens // near
    whole = lambda: pl.BlockSpec(memory_space=pltpu.VMEM)
    shape = (near * heads, length, HD)
    return pl.pallas_call(
        partial(attend_kernel, heads, ctx, near),
        out_shape=(
            jax.ShapeDtypeStruct((tokens, width), BF),
            jax.ShapeDtypeStruct((tokens, 3 * width), F32),
        ),
        in_specs=[pl.BlockSpec(memory_space=pltpu.SMEM)] + [whole() for _ in range(3)],
        out_specs=(whole(), whole()),
        scratch_shapes=[pltpu.VMEM(shape, BF)] * 4
        + [pltpu.VMEM((near * heads, HD, length), BF)] * 2
        + [pltpu.VMEM(shape, F32)] * 3,
        compiler_params=pltpu.CompilerParams(vmem_limit_bytes=60 * 1024 * 1024),
        cost_estimate=pl.CostEstimate(flops=1024, bytes_accessed=1024, transcendentals=0),
        name="attend",
    )(spot[None], pack, seg.reshape(-1, 1), seg)


def local(
    seq,
    ctx,
    hidden_in,
    segments,
    positions,
    ln1_gain,
    ln1_bias,
    ln2_gain,
    ln2_bias,
    qkv_weight,
    qkv_bias,
    out_weight,
    out_bias,
    up_weight,
    up_bias,
    down_weight,
    down_bias,
    out_grad,
):
    lay = Layout(seq, ctx)
    near, far, team = lay.near, lay.far, lay.team
    tokens, width = hidden_in.shape[1:]
    rows = qkv_weight.shape[0]
    depth = rows * team
    hidden = up_weight.shape[1]
    piece = hidden // (seq * ctx)
    share = hidden // team
    heads = H // team
    part = heads * HD
    out_rows = part // far
    cuts = depth // out_rows
    source_own = hidden_in[0]
    cotangent_own = out_grad[0]

    w_down = lay.gather_far(down_weight).reshape(share, width)

    qkv_cut = qkv_weight.reshape(rows, 3, near, ctx, part).transpose(2, 3, 0, 1, 4)
    up_cut = up_weight.reshape(rows, far, near, ctx, piece).transpose(2, 3, 0, 1, 4)
    payload = jnp.concatenate(
        [qkv_cut.reshape(near, ctx, rows, 3 * part), up_cut.reshape(near, ctx, rows, share)], 3
    )
    payload = lay.exchange_near(payload)
    source_steps = lay.beside(after(source_own, payload)), lay.across(source_own)
    small = [ln1_gain, ln1_bias, ln2_gain, ln2_bias, out_bias, down_bias, qkv_bias, up_bias]
    small = [v.astype(F32) for v in small + [segments[0], positions[0]]]
    sizes = [v.shape[0] for v in small]
    vectors = lay.gather_all(after(jnp.concatenate(small), payload))
    cut_at = [sum(sizes[:k]) for k in range(len(sizes) + 1)]
    small = [vectors[:, cut_at[k] : cut_at[k + 1]] for k in range(len(sizes))]
    seg, places = small.pop(-2), small.pop(-1)
    small = [v.reshape(-1) for v in small]
    gain_one, bias_one, gain_two, bias_two, b_out, b_down, b_qkv, b_up = small
    b_qkv = lax.dynamic_index_in_dim(b_qkv.reshape(3, team, part), lay.index, 1, keepdims=False)
    b_up = lax.dynamic_index_in_dim(b_up.reshape(far, team, piece), lay.index, 1, keepdims=False)
    seg, places = [
        lax.dynamic_index_in_dim(v.reshape(far, team, tokens), lay.far_index, 0, keepdims=False)
        for v in (seg, places)
    ]
    x_bits = jnp.arange(near)
    seg = seg.reshape(near, ctx * tokens)[x_bits ^ lay.inner].astype(jnp.int32)
    order = jnp.array([(x * ctx + k) for x, k in lay.order()])
    places = places[order ^ lay.index].reshape(-1)

    line = lambda v: v.reshape(1, -1)
    lines = [line(v) for v in (gain_two, bias_two, b_up, gain_one, bias_one, b_qkv)]

    lane = jnp.arange(part) % HD
    frequency = 10000.0 ** (-2.0 * (lane % (ROT // 2)).astype(F32) / ROT)
    frequency = jnp.where(lane < ROT, frequency, 0.0)
    theta = places[:, None] * frequency[None, :]
    cos_wide = jnp.cos(theta)
    sin_wide = jnp.where(lane < ROT // 2, -1.0, 1.0)[None, :] * jnp.sin(theta)

    payload = after(payload, vectors, source_steps[0], *source_steps[1])
    payload = lax.all_to_all(payload, "ctx", 0, 0, tiled=True)
    late = after(cotangent_own, payload)
    cotangent_steps = lay.beside(late), lay.across(late)
    payload = payload.transpose(1, 0, 2, 3).reshape(depth, -1)
    w_up = lay.gather_far(payload[:, 3 * part :]).reshape(width, share)

    source = lay.gather_team(source_own, *source_steps, 0, [w_down, cos_wide, sin_wide] + lines)
    cotangent = lay.gather_team(cotangent_own, *cotangent_steps, 1)

    out_part = lay.own_heads(after(out_weight, payload))
    out_part = out_part.reshape(out_rows, cuts, width // cuts).transpose(1, 0, 2)
    third = jnp.concatenate([payload[:, : 3 * part], out_part.reshape(depth, -1)], 1)
    third = lay.gather_far(after(third, w_up)).reshape(width, -1)

    count_all = team * tokens
    vector = jax.ShapeDtypeStruct((1, width), F32)

    hid, flow, input_one, terms, gain_two_sum, shift_two_sum, grad_up_b = by_tokens(
        partial(mlp_kernel, far),
        count_all,
        [source, cotangent],
        [],
        [w_up, w_down] + lines[:5],
        [width, width],
        [width],
        [
            jax.ShapeDtypeStruct((width, 2 * share), BF),
            vector,
            vector,
            jax.ShapeDtypeStruct((1, share), F32),
        ],
        [pltpu.VMEM((share, width), F32), pltpu.VMEM((width, share), F32)],
        "feed_forward",
    )
    terms_sum = lay.scatter_far(terms.reshape(far, depth, 2 * share))

    column = width // cuts
    packed = out_rows % 16 == 0 and column % 128 == 0
    if not packed:
        w_out = third[:, 3 * part :].reshape(far, cuts, out_rows, column)
        w_out = w_out.transpose(0, 2, 1, 3).reshape(part, width)
        third = jnp.concatenate([third[:, : 3 * part], w_out.T], 1)
    pack, w_qkv, w_out = by_tokens(
        partial(head_kernel, far if packed else 0),
        count_all,
        [cotangent],
        [input_one, cos_wide, sin_wide],
        [third, lines[5]],
        [],
        [4 * part],
        [jax.ShapeDtypeStruct((width, 3 * part), BF), jax.ShapeDtypeStruct((part, width), BF)],
        [],
        "heads",
        1024,
    )
    attended, back = attend(lay.spot, pack, seg, heads, ctx)
    (hid,) = by_tokens(
        hidden_kernel, count_all, [hid], [attended], [w_out], [width], [], [], [], "hidden", 1024
    )
    hid_got = swap(hid[1], "ctx", ctx, 1)
    linear, last, grad_qkv_b, *out_terms = by_tokens(
        partial(weights_kernel, far if packed else 0),
        count_all,
        [cotangent],
        [after(input_one, *hid), attended, back, cos_wide, sin_wide],
        [],
        [],
        [3 * part],
        [
            jax.ShapeDtypeStruct((width, 3 * part + packed * column), BF),
            jax.ShapeDtypeStruct((1, 3 * part), F32),
        ]
        + [jax.ShapeDtypeStruct((part, width), BF)] * (not packed),
        [pltpu.VMEM((width, 3 * part), F32), pltpu.VMEM((part, width), F32)],
        "weights",
        1024,
    )
    last = last.reshape(far, depth, -1)
    if not packed:
        out_terms = out_terms[0].reshape(far, out_rows, cuts, column).transpose(0, 2, 1, 3)
        last = jnp.concatenate([last, out_terms.reshape(far, depth, column)], 2)
    last_sum = lay.scatter_far(after(last, terms_sum))
    hid_first = lay.pair_blocks(after(hid[0], linear), hid_got)
    linear, flow = after((linear, tuple(flow)), terms_sum, *hid_first)
    flow, gain_one_sum, shift_one_sum = by_tokens(
        flow_kernel,
        count_all,
        [source, flow],
        [linear],
        [w_qkv, lines[3], lines[4]],
        [width],
        [],
        [vector, vector],
        [],
        "flow",
    )
    hid_came = after(lay.first_steps(hid_first), gain_one_sum)
    flow = after(tuple(flow), hid_came)
    flow_got = swap(flow[1], "ctx", ctx, 1)
    cotangent_full = cotangent_own.astype(F32)
    grad_bias = jnp.sum(cotangent_full, 0)
    mine = (jnp.arange(team) == lay.index)[None, :, None]
    grad_qkv_b = jnp.where(mine, grad_qkv_b.reshape(3, 1, part), 0.0)
    grad_up_b = jnp.where(mine, grad_up_b.reshape(far, 1, piece), 0.0)
    table = [gain_one_sum, shift_one_sum, gain_two_sum, shift_two_sum, grad_bias]
    table = [v.reshape(seq * ctx, -1) for v in table + [grad_qkv_b, grad_up_b]]
    table_all = lay.scatter_all_begin(jnp.concatenate(table, 1))

    hid_second = lay.second_steps(hid_first, hid_came)
    hid_kept = [v for pair in hid_second for v in pair if v is not None]
    flow_first = lay.pair_blocks(after(flow[0], table_all, last_sum, *hid_kept), flow_got)
    flow_came = lay.first_steps(flow_first)
    flow_second = lay.second_steps(flow_first, flow_came)
    hidden_sum = lay.last_steps(after(hid_second, flow_came))
    result = (source_own.astype(F32) + hidden_sum + (b_out + b_down)).astype(BF)[None]
    last_sum, terms_sum, table_all = after((last_sum, terms_sum, table_all), flow_second)
    flow = lay.last_steps(flow_second)

    sums = lay.scatter_all_end(table_all)
    sizes = [v.shape[1] for v in table]
    sums = [sums[sum(sizes[:k]) : sum(sizes[: k + 1])] for k in range(len(sizes))]

    last = last_sum
    both = jnp.concatenate([last[:, : 3 * part], terms_sum[:, :share]], 1)
    both = lay.exchange(both.reshape(near, ctx, rows, -1))
    grad_down_w = terms_sum[:, share:].reshape(-1, piece, share)
    grad_down_w = grad_down_w.transpose(1, 0, 2).reshape(piece, width).astype(F32)
    if part % 128 == 0 and piece % 128 == 0:
        grad_qkv_w, grad_up_w = pl.pallas_call(
            partial(unpack_kernel, far),
            out_shape=[
                jax.ShapeDtypeStruct((rows, 3 * width), F32),
                jax.ShapeDtypeStruct((rows, hidden), F32),
            ],
            in_specs=[pl.BlockSpec(memory_space=pltpu.VMEM)],
            out_specs=[pl.BlockSpec(memory_space=pltpu.VMEM)] * 2,
            cost_estimate=pl.CostEstimate(flops=1024, bytes_accessed=1024, transcendentals=0),
            name="unpack",
        )(both)
    else:
        grad_up_w = (
            both[..., 3 * part :]
            .reshape(ctx, near, rows, far, piece)
            .transpose(2, 3, 1, 0, 4)
            .reshape(rows, hidden)
            .astype(F32)
        )
        grad_qkv_w = (
            both[..., : 3 * part]
            .reshape(ctx, near, rows, 3, part)
            .transpose(2, 3, 1, 0, 4)
            .reshape(rows, 3 * width)
            .astype(F32)
        )
    out_sum = last[:, 3 * part :].reshape(cuts, out_rows, width // cuts).transpose(1, 0, 2)
    grad_out_w = lay.own_heads(out_sum.reshape(out_rows, width), back=True).astype(F32)
    wide = source_own.astype(F32)
    centred = wide - jnp.mean(wide, -1, keepdims=True)
    inverse = lax.rsqrt(jnp.mean(centred * centred, -1, keepdims=True) + EPS)
    unit = centred * inverse
    passed = (
        flow - jnp.mean(flow, -1, keepdims=True) - unit * jnp.mean(flow * unit, -1, keepdims=True)
    ) * inverse
    input_grad = (cotangent_full + passed)[None]
    return (
        result,
        input_grad,
        sums[0],
        sums[1],
        sums[2],
        sums[3],
        grad_qkv_w,
        sums[5],
        grad_out_w,
        sums[4],
        grad_up_w,
        sums[6],
        grad_down_w,
        sums[4],
    )


def solution(mesh):
    both = P(("seq", "ctx"))
    matrix = P(("seq", "ctx"), None)
    row = P("seq", "ctx", None)
    params = (both, both, both, both, matrix, both, matrix, both, matrix, both, matrix, both)
    in_specs = (row, P("seq", "ctx"), P("seq", "ctx")) + params + (row,)
    out_specs = (row, row) + params
    body = partial(local, mesh.shape["seq"], mesh.shape["ctx"])
    return jax.shard_map(body, mesh=mesh, in_specs=in_specs, out_specs=out_specs, check_vma=False)
```

```python
from functools import partial
import math

import jax
import jax.numpy as jnp
from jax import lax
from jax.experimental import pallas as pl
from jax.experimental.pallas import tpu as pltpu
from jax.sharding import PartitionSpec as P

H = 16
HD = 64
ROT = 16

EPS = 1e-05
NEG = -1000000000.0
BF = jnp.bfloat16
F32 = jnp.float32


def contract_rows(left, right):
    return lax.dot_general(left, right, (((0,), (0,)), ((), ())), preferred_element_type=F32)


def contract_cols(left, right):
    return lax.dot_general(left, right, (((1,), (1,)), ((), ())), preferred_element_type=F32)


def dot(left, right):
    return jnp.dot(left, right, preferred_element_type=F32)


def swap(value, axis, size, bits):
    return lax.ppermute(value, axis, [(i, i ^ bits) for i in range(size)])


class Layout:
    def __init__(self, seq, ctx):
        self.seq, self.ctx = seq, ctx
        self.near = 2 if seq % 2 == 0 and H % (2 * ctx) == 0 else 1
        self.far = seq // self.near
        self.team = self.near * ctx
        self.inner = lax.axis_index("seq") % self.near
        self.spot = lax.axis_index("ctx")
        self.index = self.inner * ctx + self.spot
        self.far_index = lax.axis_index("seq") // self.near
        self.groups = [[self.near * z + x for z in range(self.far)] for x in range(self.near)]

    def gather_far(self, shard):
        return lax.all_gather(shard, "seq", axis=0, axis_index_groups=self.groups)

    def scatter_far(self, terms):
        return lax.psum_scatter(
            terms, "seq", scatter_dimension=0, tiled=True, axis_index_groups=self.groups
        )[0]

    def exchange_near(self, pieces):
        if self.near == 1:
            return pieces[0][:, None]
        mine = lax.dynamic_index_in_dim(pieces, self.inner, 0, keepdims=False)
        sent = lax.dynamic_index_in_dim(pieces, 1 - self.inner, 0, keepdims=False)
        got = swap(sent, "seq", self.seq, 1)
        low = self.inner == 0
        return jnp.stack([jnp.where(low, mine, got), jnp.where(low, got, mine)], 1)

    def exchange(self, pieces):
        return lax.all_to_all(self.exchange_near(pieces), "ctx", 0, 0, tiled=True)

    def own_heads(self, value, back=False):
        pairs = []
        for z in range(self.far):
            for x in range(self.near):
                for c in range(self.ctx):
                    block = (x * self.ctx + c) * self.far + z
                    pairs.append((block, (z * self.near + x) * self.ctx + c))
        if back:
            pairs = [(b, a) for a, b in pairs]
        return lax.ppermute(value, ("seq", "ctx"), pairs)

    def gather_team(self, own, beside, across, route, first=()):
        swap_ctx = lambda v, k: swap(v, "ctx", self.ctx, k)
        if self.near == 1:
            blocks = [own] + across
        elif route == 0:
            blocks = [own, beside]
            for k, block in zip(range(2, self.ctx, 2), across):
                blocks += [block, swap_ctx(beside, k)]
        else:
            blocks = [own, beside]
            for block in across:
                blocks += [block, swap(block, "seq", self.seq, 1)]
        even = after(jnp.concatenate(blocks, 0), *first)
        return even, swap_ctx(even, 1)

    def beside(self, own):
        return swap(own, "seq", self.seq, 1) if self.near == 2 else own

    def across(self, own):
        return [swap(own, "ctx", self.ctx, k) for k in range(2, self.ctx, 2)]

    def spread(self):
        seq_bits = jnp.arange(self.seq) ^ lax.axis_index("seq")
        ctx_bits = jnp.arange(self.ctx) ^ self.spot
        return (ctx_bits[None, :] * self.seq + seq_bits[:, None]).reshape(-1)

    def gather_all(self, vector):
        table = vector[None]
        table = [table] + [swap(table, "seq", self.seq, k) for k in range(2, self.seq, 2)]
        table = jnp.concatenate(table, 0)
        table = jnp.stack([table, swap(table, "seq", self.seq, 1)], 1).reshape(self.seq, -1)
        bit = 1
        while bit < self.ctx:
            table = jnp.concatenate([table, swap(table, "ctx", self.ctx, bit)], 0)
            bit *= 2
        return table[self.spread()]

    def scatter_all_begin(self, table):
        seq_bits = jnp.arange(self.seq) ^ lax.axis_index("seq")
        ctx_bits = jnp.arange(self.ctx) ^ self.spot
        place = (seq_bits[None, :] * self.ctx + ctx_bits[:, None]).reshape(-1)
        table = table[place].reshape(self.ctx // 2, 2, self.seq, -1)
        table = table[:, 0] + swap(table[:, 1], "ctx", self.ctx, 1)
        table = table.reshape(self.ctx // 2, self.seq // 2, 2, -1)
        total = table[:, 0]
        for k in range(1, self.seq // 2):
            total = total + swap(table[:, k], "seq", self.seq, 2 * k)
        return total

    def scatter_all_end(self, table):
        table = table[:, 0] + swap(table[:, 1], "seq", self.seq, 1)
        bit = self.ctx // 4
        while bit:
            table = table[:bit] + swap(table[bit:], "ctx", self.ctx, 2 * bit)
            bit //= 2
        return table[0]

    def order(self):
        ks = list(range(0, self.ctx, 2)) + list(range(1, self.ctx, 2))
        return [(x, k) for k in ks for x in range(self.near)]

    def pair_blocks(self, even, got):
        rows = even.shape[0] * 2 // self.team
        width = even.shape[1]
        if self.near == 2 and self.ctx == 4 and width % 256 == 0:
            return list(pair_sums(even, got, rows))
        table = even.astype(F32) + got.astype(F32)
        table = table.reshape(self.ctx // 2, self.near, rows, width)
        return [table[0], table[1:].astype(BF)]

    def first_steps(self, blocks):
        came = [[swap(blocks[1][k - 1], "ctx", self.ctx, 2 * k) for k in range(1, self.ctx // 2)]]
        if len(blocks) == 4:
            came.append([swap(blocks[3], "seq", self.seq, 1)])
        return came

    def second_steps(self, blocks, came):
        result = []
        for n, values in enumerate(came):
            total = blocks[2 * n]
            for v in values:
                total = total + v.astype(F32)
            result.append((total[0], total[1].astype(BF)) if self.near == 2 else (total[0], None))
        return result

    def last_steps(self, steps):
        if self.near == 1:
            return steps[0][0]
        parts = [steps[0][0] + swap(steps[0][1], "seq", self.seq, 1).astype(F32)]
        if len(steps) == 2:
            parts.append(steps[1][0] + swap(steps[1][1], "ctx", self.ctx, 2).astype(F32))
        return jnp.concatenate(parts, 1)


def after(value, *first):
    return lax.optimization_barrier((value,) + first)[0]


def normed(value, gain, shift):
    wide = value.astype(F32)
    centred = wide - jnp.mean(wide, -1, keepdims=True)
    unit = centred * lax.rsqrt(jnp.mean(centred * centred, -1, keepdims=True) + EPS)
    return unit, (unit * gain + shift).astype(BF)


def turn(u, cosine, sine):
    width = u.shape[-1]
    lane = lax.broadcasted_iota(jnp.int32, u.shape, 1) % HD
    moved = jnp.where(
        lane < ROT // 2, pltpu.roll(u, width - ROT // 2, 1), pltpu.roll(u, ROT // 2, 1)
    )
    return u * cosine + moved * sine


def row_sum(value):
    return jnp.sum(value, 0, keepdims=True)


def pack_rows(target, start, size, source, peers):
    rows = source.shape[0] // peers
    depth = target.shape[0] // peers
    for z in range(peers):
        for n in range(source.shape[1] // size):
            at = pl.ds(z * depth + n * rows, rows)
            piece = source[pl.ds(z * rows, rows), pl.ds(n * size, size)]
            target[at, pl.ds(start, size)] = piece.astype(BF)


def mlp_kernel(
    peers, x_ref, g_ref, up_ref, down_ref, gain_ref, shift_ref, bias_ref, gain_one_ref, shift_one_ref,
    hid_ref, flow_ref, one_ref, terms_out, gain_out, shift_out, bias_out,
    down_s, up_s, unit_s, value_s, active_s, grad_s,
):
    step = pl.program_id(0)

    @pl.when(step == 0)
    def _():
        for ref in (down_s, up_s, gain_out, shift_out, bias_out):
            ref[...] = jnp.zeros_like(ref)

    gain, shift = gain_ref[...], shift_ref[...]
    gain_one, shift_one = gain_one_ref[...], shift_one_ref[...]
    for at in chunks(value_s.shape[0]):
        unit, value = normed(load(x_ref, at), gain, shift)
        unit_s[at, :] = unit
        value_s[at, :] = value
        one_ref[at, :] = (unit * gain_one + shift_one).astype(BF)
    value, grad = value_s[...], load(g_ref)
    upper = dot(value, up_ref[...])
    grad_active = contract_cols(grad, down_ref[...])
    bias = bias_ref[...]
    for at in chunks(value_s.shape[0]):
        u = upper[at] + bias
        cdf = 0.5 * (1.0 + lax.erf(u * math.sqrt(0.5)))
        density = jnp.exp(-0.5 * u * u) * (1.0 / math.sqrt(2.0 * math.pi))
        active_s[at, :] = (u * cdf).astype(BF)
        low = (grad_active[at] * (cdf + u * density)).astype(BF)
        grad_s[at, :] = low
        bias_out[...] += row_sum(low.astype(F32))
    active, grad_upper = active_s[...], grad_s[...]
    store(hid_ref, dot(active, down_ref[...]).astype(BF))
    down_s[...] += contract_rows(active, grad)
    up_s[...] += contract_rows(value, grad_upper)
    back = contract_cols(grad_upper, up_ref[...])
    flows = []
    for at in chunks(value_s.shape[0]):
        part = back[at]
        flows.append((part * gain).astype(BF))
        gain_out[...] += row_sum(part * unit_s[at, :])
        shift_out[...] += row_sum(part)
    store(flow_ref, jnp.concatenate(flows, 0))

    @pl.when(step == pl.num_programs(0) - 1)
    def _():
        share = up_s.shape[1]
        terms_out[:, 0:share] = up_s[...].astype(BF)
        pack_rows(terms_out, share, share, down_s, peers)


def head_kernel(
    peers, g_ref, value_ref, cos_ref, sin_ref, third_ref, bias_ref, pack_ref, qkv_ref, out_ref
):
    @pl.when(pl.program_id(0) == 0)
    def _():
        size = third_ref.shape[1] - qkv_ref.shape[1]
        depth, rows = [v.shape[0] // max(peers, 1) for v in (third_ref, out_ref)]
        qkv_ref[...] = third_ref[:, 0 : qkv_ref.shape[1]]
        if not peers:
            out_ref[...] = third_ref[:, qkv_ref.shape[1] :].T
        for z in range(peers):
            for n in range(out_ref.shape[1] // size):
                at = pl.ds(z * depth + n * rows, rows)
                piece = third_ref[at, pl.ds(qkv_ref.shape[1], size)]
                out_ref[pl.ds(z * rows, rows), pl.ds(n * size, size)] = piece

    width = cos_ref.shape[1]
    linear = dot(value_ref[...], qkv_ref[...]) + bias_ref[...]
    cosine, sine = cos_ref[...], sin_ref[...]
    scale = 1.0 / math.sqrt(HD)
    query = turn(linear[:, 0:width], cosine, sine) * scale
    pack_ref[:, 0:width] = query.astype(BF)
    pack_ref[:, width : 2 * width] = turn(linear[:, width : 2 * width], cosine, sine).astype(BF)
    pack_ref[:, 2 * width : 3 * width] = linear[:, 2 * width : 3 * width].astype(BF)
    pack_ref[:, 3 * width : 4 * width] = contract_cols(load(g_ref), out_ref[...]).astype(BF)


def weights_kernel(
    peers, g_ref, value_ref, att_ref, back_ref, cos_ref, sin_ref,
    linear_out, terms_out, bias_out, *rest
):
    *out_out, qkv_s, out_s = rest
    step = pl.program_id(0)
    width = cos_ref.shape[1]

    @pl.when(step == 0)
    def _():
        for ref in (qkv_s, out_s, bias_out):
            ref[...] = jnp.zeros_like(ref)

    cosine, sine = cos_ref[...], -sin_ref[...]
    scale = 1.0 / math.sqrt(HD)
    linear = jnp.concatenate(
        [
            turn(back_ref[:, 0:width] * scale, cosine, sine),
            turn(back_ref[:, width : 2 * width], cosine, sine),
            back_ref[:, 2 * width : 3 * width],
        ],
        -1,
    ).astype(BF)
    linear_out[...] = linear
    qkv_s[...] += contract_rows(value_ref[...], linear)
    out_s[...] += contract_rows(att_ref[...], load(g_ref))
    bias_out[...] += row_sum(linear.astype(F32))

    @pl.when(step == pl.num_programs(0) - 1)
    def _():
        terms_out[:, 0 : 3 * width] = qkv_s[...].astype(BF)
        if peers:
            pack_rows(terms_out, 3 * width, terms_out.shape[1] - 3 * width, out_s, peers)
        else:
            out_out[0][...] = out_s[...].astype(BF)


def flow_kernel(
    x_ref, flow_ref, linear_ref, qkv_ref, gain_ref, shift_ref, flow_out, gain_out, shift_out
):
    @pl.when(pl.program_id(0) == 0)
    def _():
        for ref in (gain_out, shift_out):
            ref[...] = jnp.zeros_like(ref)

    gain, shift = gain_ref[...], shift_ref[...]
    back = contract_cols(linear_ref[...], qkv_ref[...])
    flows = []
    for at in chunks(back.shape[0]):
        part = back[at]
        unit, _ = normed(load(x_ref, at), gain, shift)
        flows.append((load(flow_ref, at).astype(F32) + part * gain).astype(BF))
        gain_out[...] += row_sum(part * unit)
        shift_out[...] += row_sum(part)
    store(flow_out, jnp.concatenate(flows, 0))


def hidden_kernel(hid_ref, att_ref, out_ref, hid_out):
    store(hid_out, (load(hid_ref).astype(F32) + dot(att_ref[...], out_ref[...])).astype(BF))


def pair_kernel(rows, even_ref, got_ref, left_ref, left_sent, right_ref, right_sent):
    half = even_ref.shape[1] // 2
    for k in range(4):
        at = pl.ds(k * rows, rows)
        total = even_ref[at, :].astype(F32) + got_ref[at, :].astype(F32)
        left, right = total[:, :half], total[:, half:]
        if k < 2:
            left_ref[k] = left
        else:
            left_sent[0, k - 2] = left.astype(BF)
        if k % 2 == 0:
            right_ref[k // 2] = right
        else:
            right_sent[k // 2] = right.astype(BF)


def pair_sums(even, got, rows):
    shape = (2, rows, even.shape[1] // 2)
    return pl.pallas_call(
        partial(pair_kernel, rows),
        out_shape=[
            jax.ShapeDtypeStruct(shape, F32),
            jax.ShapeDtypeStruct((1,) + shape, BF),
            jax.ShapeDtypeStruct(shape, F32),
            jax.ShapeDtypeStruct(shape, BF),
        ],
        in_specs=[pl.BlockSpec(memory_space=pltpu.VMEM)] * 2,
        out_specs=[pl.BlockSpec(memory_space=pltpu.VMEM)] * 4,
        compiler_params=pltpu.CompilerParams(vmem_limit_bytes=60 * 1024 * 1024),
        cost_estimate=pl.CostEstimate(flops=1024, bytes_accessed=1024, transcendentals=0),
        name="pair_sums",
    )(even, got)


def unpack_kernel(far, both_ref, qkv_ref, up_ref):
    ctx, near = both_ref.shape[:2]
    team = ctx * near
    part, piece = qkv_ref.shape[1] // (3 * team), up_ref.shape[1] // (far * team)
    for c in range(ctx):
        for x in range(near):
            value = both_ref[c, x].astype(F32)
            for n in range(3):
                at = (n * team + x * ctx + c) * part
                qkv_ref[:, at : at + part] = value[:, n * part : (n + 1) * part]
            for z in range(far):
                at = (z * team + x * ctx + c) * piece
                low = 3 * part + z * piece
                up_ref[:, at : at + piece] = value[:, low : low + piece]


def first_half():
    return pl.program_id(0) < pl.num_programs(0) // 2


def chunks(rows):
    size = math.gcd(rows, 64)
    return [slice(start, start + size) for start in range(0, rows, size)]


def load(pair, at=slice(None)):
    return jnp.where(first_half(), pair[0][at, :], pair[1][at, :])


def store(pair, value):
    @pl.when(first_half())
    def _():
        pair[0][...] = value

    @pl.when(jnp.logical_not(first_half()))
    def _():
        pair[1][...] = value


def by_tokens(kernel, tokens, pairs, streamed, fixed, pairs_out, streamed_out, fixed_out, scratch, name, size=512, limit=52):
    block = math.gcd(tokens // 2, size)
    steps = tokens // block
    stream = lambda n: pl.BlockSpec((block, n), lambda i: (i, 0))
    whole = lambda shape: pl.BlockSpec(shape, lambda i: (0, 0))
    halves = lambda n: [
        pl.BlockSpec((block, n), lambda i: (jnp.minimum(i, steps // 2 - 1), 0)),
        pl.BlockSpec((block, n), lambda i: (jnp.maximum(i - steps // 2, 0), 0)),
    ]
    counts = [2] * len(pairs) + [1] * (len(streamed) + len(fixed))
    counts += [2] * len(pairs_out) + [1] * (len(streamed_out) + len(fixed_out) + len(scratch))

    def body(*refs):
        refs, given = list(refs), []
        for count in counts:
            given.append(refs.pop(0) if count == 1 else (refs.pop(0), refs.pop(0)))
        kernel(*given)

    inputs = [v for pair in pairs for v in pair] + list(streamed) + list(fixed)
    outputs = [jax.ShapeDtypeStruct((tokens // 2, n), BF) for n in pairs_out for _ in range(2)]
    outputs += [jax.ShapeDtypeStruct((tokens, n), BF) for n in streamed_out] + list(fixed_out)
    result = pl.pallas_call(
        body,
        grid=(steps,),
        in_specs=[spec for pair in pairs for spec in halves(pair[0].shape[1])]
        + [stream(v.shape[1]) for v in streamed]
        + [whole(v.shape) for v in fixed],
        out_specs=[spec for n in pairs_out for spec in halves(n)]
        + [stream(n) for n in streamed_out]
        + [whole(v.shape) for v in fixed_out],
        out_shape=outputs,
        scratch_shapes=scratch,
        compiler_params=pltpu.CompilerParams(vmem_limit_bytes=limit * 1024 * 1024),
        cost_estimate=pl.CostEstimate(flops=1024, bytes_accessed=1024, transcendentals=0),
        name=name,
    )(*inputs)
    result, given = list(result), []
    for count in [2] * len(pairs_out) + [1] * (len(streamed_out) + len(fixed_out)):
        given.append(result.pop(0) if count == 1 else (result.pop(0), result.pop(0)))
    return given


def attend_kernel(
    heads, ctx, near,
    spot_ref, pack_ref, seg_col_ref, seg_row_ref,
    out_ref, back_ref,
    q_s, k_s, v_s, g_s, kt_s, vt_s, dq_s, dk_s, dv_s,
):
    length = pack_ref.shape[0] // near
    width = out_ref.shape[1]
    rows = length // ctx
    block = math.gcd(rows, 256)
    spot = spot_ref[0]

    def place(i, x):
        other = spot ^ i
        return pl.multiple_of((((other >> 1) + (other & 1) * (ctx // 2)) * near + x) * rows, rows)

    def prepare(step, carry):
        i, x = step // near, step % near
        pack = pack_ref[pl.ds(place(i, x), rows), :]
        for n, target in enumerate((q_s, k_s, v_s, g_s)):
            for h in range(heads):
                low = n * width + h * HD
                target[x * heads + h, pl.ds(i * rows, rows), :] = pack[:, low : low + HD]
        return carry

    lax.fori_loop(0, ctx * near, prepare, 0)
    def one(h, start, size):
        at = pl.ds(start, block)
        query, grad = q_s[h, at, :], g_s[h, at, :]
        keys, values = k_s[h, 0:size, :], v_s[h, 0:size, :]
        scores = contract_cols(keys, query)
        row = lax.broadcasted_iota(jnp.int32, (size, block), 0)
        col = start + lax.broadcasted_iota(jnp.int32, (size, block), 1)
        x = h // heads
        seg_col = seg_col_ref[pl.ds(x * length, size), :]
        seg_row = seg_row_ref[pl.ds(x, 1), at]
        scores = jnp.where((seg_col == seg_row) & (row <= col), scores, NEG)
        raw = jnp.exp(scores - jnp.max(scores, 0, keepdims=True))
        prob = raw * (1.0 / jnp.sum(raw, 0, keepdims=True))
        prob_low = prob.astype(BF)
        grad_prob = contract_cols(values, grad)
        delta = jnp.sum(prob * grad_prob, 0, keepdims=True)
        grad_score = (prob * (grad_prob - delta)).astype(BF)
        dv_s[h, 0:size, :] += dot(prob_low, grad)
        dk_s[h, 0:size, :] += dot(grad_score, query)
        dq_s[h, at, :] = dot(kt_s[h, :, 0:size], grad_score).T
        q_s[h, at, :] = dot(vt_s[h, :, 0:size], prob_low).T.astype(BF)

    def flip(h, carry):
        kt_s[h] = k_s[h].T
        vt_s[h] = v_s[h].T
        return carry

    lax.fori_loop(0, near * heads, flip, 0)

    count = length // block
    if count <= 4:

        def each(h, carry):
            x = h // heads
            ats = [pl.ds(i * block, block) for i in range(count)]
            queries, grads = [q_s[h, at, :] for at in ats], [g_s[h, at, :] for at in ats]
            keys, values = k_s[h], v_s[h]
            seg_col = seg_col_ref[pl.ds(pl.multiple_of(x * length, block), length), :]
            seg_row = seg_row_ref[pl.ds(x, 1), :]
            row = lax.broadcasted_iota(jnp.int32, (block, block), 0)
            col = lax.broadcasted_iota(jnp.int32, (block, block), 1)
            scores = [
                contract_cols(keys[: (i + 1) * block], query) for i, query in enumerate(queries)
            ]
            grad_probs = [
                contract_cols(values[: (i + 1) * block], grad) for i, grad in enumerate(grads)
            ]
            probs, grad_scores = [], []
            for i in range(count):
                size = (i + 1) * block
                same = seg_col[:size] == seg_row[:, i * block : size]
                score = jnp.where(same, scores[i], NEG)
                last = jnp.where(row <= col, score[i * block :], NEG)
                score = jnp.concatenate([score[: i * block], last], 0) if i else last
                raw = jnp.exp(score - jnp.max(score, 0, keepdims=True))
                prob = raw * (1.0 / jnp.sum(raw, 0, keepdims=True))
                delta = jnp.sum(prob * grad_probs[i], 0, keepdims=True)
                probs.append(prob.astype(BF))
                grad_scores.append((prob * (grad_probs[i] - delta)).astype(BF))
            for i, at in enumerate(ats):
                size = (i + 1) * block
                dq_s[h, at, :] = dot(kt_s[h, :, 0:size], grad_scores[i]).T
                q_s[h, at, :] = dot(vt_s[h, :, 0:size], probs[i]).T.astype(BF)
            for j, at in enumerate(ats):
                low = slice(j * block, (j + 1) * block)
                dv_s[h, at, :] = sum(dot(probs[i][low], grads[i]) for i in range(j, count))
                dk_s[h, at, :] = sum(dot(grad_scores[i][low], queries[i]) for i in range(j, count))
            return carry

        lax.fori_loop(0, near * heads, each, 0)
    else:
        dk_s[...] = jnp.zeros_like(dk_s)
        dv_s[...] = jnp.zeros_like(dv_s)

        def each(step, carry):
            one(step // count, pl.multiple_of(step % count * block, block), length)
            return carry

        lax.fori_loop(0, near * heads * count, each, 0)

    def finish(step, carry):
        i, x = step // near, step % near
        at = pl.ds(place(i, x), rows)

        def join(source):
            return jnp.concatenate(
                [source[x * heads + h, pl.ds(i * rows, rows), :] for h in range(heads)], -1
            )

        out_ref[at, :] = join(q_s)
        for n, source in enumerate((dq_s, dk_s, dv_s)):
            back_ref[at, n * width : (n + 1) * width] = join(source)
        return carry

    lax.fori_loop(0, ctx * near, finish, 0)


def attend(spot, pack, seg, heads, ctx):
    near = seg.shape[0]
    tokens, width = pack.shape[0], pack.shape[1] // 4
    length = tokens // near
    whole = lambda: pl.BlockSpec(memory_space=pltpu.VMEM)
    shape = (near * heads, length, HD)
    return pl.pallas_call(
        partial(attend_kernel, heads, ctx, near),
        out_shape=(
            jax.ShapeDtypeStruct((tokens, width), BF),
            jax.ShapeDtypeStruct((tokens, 3 * width), F32),
        ),
        in_specs=[pl.BlockSpec(memory_space=pltpu.SMEM)] + [whole() for _ in range(3)],
        out_specs=(whole(), whole()),
        scratch_shapes=[pltpu.VMEM(shape, BF)] * 4
        + [pltpu.VMEM((near * heads, HD, length), BF)] * 2
        + [pltpu.VMEM(shape, F32)] * 3,
        compiler_params=pltpu.CompilerParams(vmem_limit_bytes=48 * 1024 * 1024),
        cost_estimate=pl.CostEstimate(flops=1024, bytes_accessed=1024, transcendentals=0),
        name="attend",
    )(spot[None], pack, seg.reshape(-1, 1), seg)


def local(
    seq,
    ctx,
    hidden_in,
    segments,
    positions,
    ln1_gain,
    ln1_bias,
    ln2_gain,
    ln2_bias,
    qkv_weight,
    qkv_bias,
    out_weight,
    out_bias,
    up_weight,
    up_bias,
    down_weight,
    down_bias,
    out_grad,
):
    lay = Layout(seq, ctx)
    near, far, team = lay.near, lay.far, lay.team
    tokens, width = hidden_in.shape[1:]
    rows = qkv_weight.shape[0]
    depth = rows * team
    hidden = up_weight.shape[1]
    piece = hidden // (seq * ctx)
    share = hidden // team
    heads = H // team
    part = heads * HD
    out_rows = part // far
    cuts = depth // out_rows
    source_own = hidden_in[0]
    cotangent_own = out_grad[0]

    w_down = lay.gather_far(down_weight).reshape(share, width)

    qkv_cut = qkv_weight.reshape(rows, 3, near, ctx, part).transpose(2, 3, 0, 1, 4)
    up_cut = up_weight.reshape(rows, far, near, ctx, piece).transpose(2, 3, 0, 1, 4)
    payload = jnp.concatenate(
        [qkv_cut.reshape(near, ctx, rows, 3 * part), up_cut.reshape(near, ctx, rows, share)], 3
    )
    payload = lay.exchange_near(payload)
    source_steps = lay.beside(after(source_own, payload)), lay.across(source_own)
    small = [ln1_gain, ln1_bias, ln2_gain, ln2_bias, out_bias, down_bias, qkv_bias, up_bias]
    small = [v.astype(F32) for v in small + [segments[0], positions[0]]]
    sizes = [v.shape[0] for v in small]
    vectors = lay.gather_all(after(jnp.concatenate(small), payload))
    cut_at = [sum(sizes[:k]) for k in range(len(sizes) + 1)]
    small = [vectors[:, cut_at[k] : cut_at[k + 1]] for k in range(len(sizes))]
    seg, places = small.pop(-2), small.pop(-1)
    small = [v.reshape(-1) for v in small]
    gain_one, bias_one, gain_two, bias_two, b_out, b_down, b_qkv, b_up = small
    b_qkv = lax.dynamic_index_in_dim(b_qkv.reshape(3, team, part), lay.index, 1, keepdims=False)
    b_up = lax.dynamic_index_in_dim(b_up.reshape(far, team, piece), lay.index, 1, keepdims=False)
    seg, places = [
        lax.dynamic_index_in_dim(v.reshape(far, team, tokens), lay.far_index, 0, keepdims=False)
        for v in (seg, places)
    ]
    x_bits = jnp.arange(near)
    seg = seg.reshape(near, ctx * tokens)[x_bits ^ lay.inner].astype(jnp.int32)
    order = jnp.array([(x * ctx + k) for x, k in lay.order()])
    places = places[order ^ lay.index].reshape(-1)

    line = lambda v: v.reshape(1, -1)
    lines = [line(v) for v in (gain_two, bias_two, b_up, gain_one, bias_one, b_qkv)]

    lane = jnp.arange(part) % HD
    frequency = 10000.0 ** (-2.0 * (lane % (ROT // 2)).astype(F32) / ROT)
    frequency = jnp.where(lane < ROT, frequency, 0.0)
    theta = places[:, None] * frequency[None, :]
    cos_wide = jnp.cos(theta)
    sin_wide = jnp.where(lane < ROT // 2, -1.0, 1.0)[None, :] * jnp.sin(theta)

    payload = after(payload, vectors, source_steps[0], *source_steps[1])
    payload = lax.all_to_all(payload, "ctx", 0, 0, tiled=True)
    late = after(cotangent_own, payload)
    cotangent_steps = lay.beside(late), lay.across(late)
    payload = payload.transpose(1, 0, 2, 3).reshape(depth, -1)
    w_up = lay.gather_far(payload[:, 3 * part :]).reshape(width, share)

    source = lay.gather_team(source_own, *source_steps, 0, [w_down, cos_wide, sin_wide] + lines)
    cotangent = lay.gather_team(cotangent_own, *cotangent_steps, 1)

    out_part = lay.own_heads(after(out_weight, payload))
    out_part = out_part.reshape(out_rows, cuts, width // cuts).transpose(1, 0, 2)
    third = jnp.concatenate([payload[:, : 3 * part], out_part.reshape(depth, -1)], 1)
    third = lay.gather_far(after(third, w_up)).reshape(width, -1)

    count_all = team * tokens
    vector = jax.ShapeDtypeStruct((1, width), F32)

    block = math.gcd(count_all // 2, 512)
    hid, flow, input_one, terms, gain_two_sum, shift_two_sum, grad_up_b = by_tokens(
        partial(mlp_kernel, far),
        count_all,
        [source, cotangent],
        [],
        [w_up, w_down] + lines[:5],
        [width, width],
        [width],
        [
            jax.ShapeDtypeStruct((width, 2 * share), BF),
            vector,
            vector,
            jax.ShapeDtypeStruct((1, share), F32),
        ],
        [pltpu.VMEM((share, width), F32), pltpu.VMEM((width, share), F32)]
        + [pltpu.VMEM((block, width), t) for t in (F32, BF)]
        + [pltpu.VMEM((block, share), BF)] * 2,
        "feed_forward",
        limit=60,
    )
    terms_sum = lay.scatter_far(terms.reshape(far, depth, 2 * share))

    column = width // cuts
    packed = out_rows % 16 == 0 and column % 128 == 0
    if not packed:
        w_out = third[:, 3 * part :].reshape(far, cuts, out_rows, column)
        w_out = w_out.transpose(0, 2, 1, 3).reshape(part, width)
        third = jnp.concatenate([third[:, : 3 * part], w_out.T], 1)
    pack, w_qkv, w_out = by_tokens(
        partial(head_kernel, far if packed else 0),
        count_all,
        [cotangent],
        [input_one, cos_wide, sin_wide],
        [third, lines[5]],
        [],
        [4 * part],
        [jax.ShapeDtypeStruct((width, 3 * part), BF), jax.ShapeDtypeStruct((part, width), BF)],
        [],
        "heads",
    )
    attended, back = attend(lay.spot, pack, seg, heads, ctx)
    (hid,) = by_tokens(
        hidden_kernel, count_all, [hid], [attended], [w_out], [width], [], [], [], "hidden"
    )
    hid_got = swap(hid[1], "ctx", ctx, 1)
    linear, last, grad_qkv_b, *out_terms = by_tokens(
        partial(weights_kernel, far if packed else 0),
        count_all,
        [cotangent],
        [after(input_one, *hid), attended, back, cos_wide, sin_wide],
        [],
        [],
        [3 * part],
        [
            jax.ShapeDtypeStruct((width, 3 * part + packed * column), BF),
            jax.ShapeDtypeStruct((1, 3 * part), F32),
        ]
        + [jax.ShapeDtypeStruct((part, width), BF)] * (not packed),
        [pltpu.VMEM((width, 3 * part), F32), pltpu.VMEM((part, width), F32)],
        "weights",
    )
    last = last.reshape(far, depth, -1)
    if not packed:
        out_terms = out_terms[0].reshape(far, out_rows, cuts, column).transpose(0, 2, 1, 3)
        last = jnp.concatenate([last, out_terms.reshape(far, depth, column)], 2)
    last_sum = lay.scatter_far(after(last, terms_sum))
    hid_first = lay.pair_blocks(after(hid[0], linear), hid_got)
    linear, flow = after((linear, tuple(flow)), terms_sum, *hid_first)
    flow, gain_one_sum, shift_one_sum = by_tokens(
        flow_kernel,
        count_all,
        [source, flow],
        [linear],
        [w_qkv, lines[3], lines[4]],
        [width],
        [],
        [vector, vector],
        [],
        "flow",
        limit=60,
    )
    hid_came = after(lay.first_steps(hid_first), gain_one_sum)
    flow = after(tuple(flow), hid_came)
    flow_got = swap(flow[1], "ctx", ctx, 1)
    cotangent_full = cotangent_own.astype(F32)
    grad_bias = jnp.sum(cotangent_full, 0)
    mine = (jnp.arange(team) == lay.index)[None, :, None]
    grad_qkv_b = jnp.where(mine, grad_qkv_b.reshape(3, 1, part), 0.0)
    grad_up_b = jnp.where(mine, grad_up_b.reshape(far, 1, piece), 0.0)
    table = [gain_one_sum, shift_one_sum, gain_two_sum, shift_two_sum, grad_bias]
    table = [v.reshape(seq * ctx, -1) for v in table + [grad_qkv_b, grad_up_b]]
    table_all = lay.scatter_all_begin(jnp.concatenate(table, 1))

    hid_second = lay.second_steps(hid_first, hid_came)
    hid_kept = [v for pair in hid_second for v in pair if v is not None]
    flow_first = lay.pair_blocks(after(flow[0], table_all, last_sum, *hid_kept), flow_got)
    flow_came = lay.first_steps(flow_first)
    flow_second = lay.second_steps(flow_first, flow_came)
    hidden_sum = lay.last_steps(after(hid_second, flow_came))
    result = (source_own.astype(F32) + hidden_sum + (b_out + b_down)).astype(BF)[None]
    last_sum, terms_sum, table_all = after((last_sum, terms_sum, table_all), flow_second)
    flow = lay.last_steps(flow_second)

    sums = lay.scatter_all_end(table_all)
    sizes = [v.shape[1] for v in table]
    sums = [sums[sum(sizes[:k]) : sum(sizes[: k + 1])] for k in range(len(sizes))]

    last = last_sum
    both = jnp.concatenate([last[:, : 3 * part], terms_sum[:, :share]], 1)
    both = lay.exchange(both.reshape(near, ctx, rows, -1))
    grad_down_w = terms_sum[:, share:].reshape(-1, piece, share)
    grad_down_w = grad_down_w.transpose(1, 0, 2).reshape(piece, width).astype(F32)
    if part % 128 == 0 and piece % 128 == 0:
        grad_qkv_w, grad_up_w = pl.pallas_call(
            partial(unpack_kernel, far),
            out_shape=[
                jax.ShapeDtypeStruct((rows, 3 * width), F32),
                jax.ShapeDtypeStruct((rows, hidden), F32),
            ],
            in_specs=[pl.BlockSpec(memory_space=pltpu.VMEM)],
            out_specs=[pl.BlockSpec(memory_space=pltpu.VMEM)] * 2,
            cost_estimate=pl.CostEstimate(flops=1024, bytes_accessed=1024, transcendentals=0),
            name="unpack",
        )(both)
    else:
        grad_up_w = (
            both[..., 3 * part :]
            .reshape(ctx, near, rows, far, piece)
            .transpose(2, 3, 1, 0, 4)
            .reshape(rows, hidden)
            .astype(F32)
        )
        grad_qkv_w = (
            both[..., : 3 * part]
            .reshape(ctx, near, rows, 3, part)
            .transpose(2, 3, 1, 0, 4)
            .reshape(rows, 3 * width)
            .astype(F32)
        )
    out_sum = last[:, 3 * part :].reshape(cuts, out_rows, width // cuts).transpose(1, 0, 2)
    grad_out_w = lay.own_heads(out_sum.reshape(out_rows, width), back=True).astype(F32)
    wide = source_own.astype(F32)
    centred = wide - jnp.mean(wide, -1, keepdims=True)
    inverse = lax.rsqrt(jnp.mean(centred * centred, -1, keepdims=True) + EPS)
    unit = centred * inverse
    passed = (
        flow - jnp.mean(flow, -1, keepdims=True) - unit * jnp.mean(flow * unit, -1, keepdims=True)
    ) * inverse
    input_grad = (cotangent_full + passed)[None]
    return (
        result,
        input_grad,
        sums[0],
        sums[1],
        sums[2],
        sums[3],
        grad_qkv_w,
        sums[5],
        grad_out_w,
        sums[4],
        grad_up_w,
        sums[6],
        grad_down_w,
        sums[4],
    )


def solution(mesh):
    both = P(("seq", "ctx"))
    matrix = P(("seq", "ctx"), None)
    row = P("seq", "ctx", None)
    params = (both, both, both, both, matrix, both, matrix, both, matrix, both, matrix, both)
    in_specs = (row, P("seq", "ctx"), P("seq", "ctx")) + params + (row,)
    out_specs = (row, row) + params
    body = partial(local, mesh.shape["seq"], mesh.shape["ctx"])
    return jax.shard_map(body, mesh=mesh, in_specs=in_specs, out_specs=out_specs, check_vma=False)
```
